128 devices in a mesh: rows: 32 (over y, x, z_hi), disp: 4 (over z_lo, core).
Axes of the slice: x: 4, y: 4, z: 4 (z_hi: 2, z_lo: 2; z = z_hi * 2 + z_lo), core: 2. Of those that a mesh axis runs over, the one named last changes fastest.
Arguments:
- left_features: bfloat16 [1, 64, 224, 256], P(None, 'rows'), may hold values from -6 to 6
- right_features: bfloat16 [1, 64, 224, 256], P(None, 'rows'), may hold values from -6 to 6
- stem_weights: bfloat16 [32, 8], replicated, may hold values from -2 to 2
- conv_weights: bfloat16 [2, 32, 3, 3, 3, 32], replicated, may hold values from -0.21875 to 0.21875
- attn_weights: bfloat16 [3, 32, 32], replicated, may hold values from -6 to 6
- head: float32 [32], replicated, may hold values from -1.5 to 1.5
- target_disparity: float32 [1, 64, 256], P(None, 'rows'), may hold values from 0 to 103
Outputs:
- disparity: float32 [1, 64, 256], P(None, 'rows')
- normals: float32 [3, 1, 64, 256], P(None, None, 'rows')
- loss: float32 [], replicated
- head_grad: float32 [32], replicated
The draws below stay inside these ranges and needn't reach their ends.
All inputs are finite; a program needn't handle non-finite values.
Results may differ from the reference program's by a relative error of at most 0.03225.
Values may be sent and summed in bfloat16 or wider, within the bound.
No kernel may reach another device: no remote copies, remote signals or barrier semaphores. Data moves between devices by JAX's collectives and lax.ppermute only.
A program may use at most 64 MiB of HBM per device.

```python
import math
import jax
import jax.numpy as jnp
from jax import lax

C = 224
G = 8
V = 32
DISP = 104
W = 256
BATCH = 1
LAYERS = 2
H = 64


def draw_attn_weights(key, part):
    key = jax.random.fold_in(key, 11)
    base = jax.random.truncated_normal(key, -3.0, 3.0, (3, V, V), jnp.float32) * (2.0 / math.sqrt(V))
    return base.astype(jnp.bfloat16)


def draw_head(key, part):
    key = jax.random.fold_in(key, 12)
    return jax.random.truncated_normal(key, -3.0, 3.0, (V,), jnp.float32) * 0.5


def steps_of(rng, dims, split, least, high):
    def one(dim, blocks):
        steps = jax.random.uniform(jax.random.fold_in(jax.random.fold_in(rng, 6), dim), (blocks,), jnp.float32, least / len(split), high / len(split))
        return jnp.repeat(jnp.exp(steps), dims[dim] // blocks).reshape((-1,) + (1,) * (len(dims) - dim - 1))

    loudness = one(*split[0])
    for cut in split[1:]:
        loudness = loudness * one(*cut)
    return loudness


def normal_values(stream_key, shape, scale, most, cuts=(), kind=jnp.bfloat16):
    drawn = scale * jax.random.normal(stream_key, shape, jnp.float32)
    if cuts:
        drawn = drawn * steps_of(stream_key, shape, cuts, -0.22, 0.18)
    return jnp.clip(drawn, -most, most).astype(kind)


def setup_inputs(seed: int = 0) -> dict:
    splits = jax.random.split(jax.random.key(seed), 8)
    return {
        "left_features": normal_values(splits[0], (BATCH, H, C, W), 1.0, 6.0, ((1, 32),)),
        "right_features": normal_values(splits[1], (BATCH, H, C, W), 1.0, 6.0, ((1, 32),)),
        "stem_weights": normal_values(splits[2], (V, G), G ** -0.5, 2.0),
        "conv_weights": normal_values(splits[3], (LAYERS, V, 3, 3, 3, V), (27 * V) ** -0.5, 0.21875),
        "attn_weights": draw_attn_weights(jax.random.fold_in(splits[7], 71), 0),
        "head": draw_head(jax.random.fold_in(splits[7], 71), 0),
        "target_disparity": jnp.clip(103.0 * jax.random.uniform(splits[6], (BATCH, H, W), jnp.float32) ** steps_of(splits[6], (BATCH, H, W), ((1, 32),), -0.2, 0.2), 0.0, 103.0),
    }


def correlate(left_features, right_pad, shift_list, offset, col_count):
    images, band_rows, channels, _ = left_features.shape
    width_group = channels // G
    left_cols = lax.dynamic_slice_in_dim(left_features, offset, col_count, 3)

    def single(shift_by):
        moved = lax.dynamic_slice_in_dim(right_pad, offset + DISP - shift_by, col_count, 3)
        product = left_cols.astype(jnp.float32) * moved.astype(jnp.float32)
        summed = product.reshape(images, band_rows, G, width_group, col_count).sum(3) / width_group
        return summed.astype(jnp.bfloat16)
    stacked = lax.map(single, shift_list)
    return stacked.transpose(1, 3, 0, 2, 4)

def lift(cost_volume, stem_weights):
    return jnp.einsum('vg,bgdhw->bvdhw', stem_weights.astype(jnp.float32), cost_volume.astype(jnp.float32), precision=lax.Precision.HIGHEST).astype(jnp.bfloat16)

def convolve(volume, kernel):
    padded = jnp.pad(volume, ((0, 0), (0, 0), (1, 1), (1, 1), (1, 1)))
    depth_len, row_count, col_count = (volume.shape[2], volume.shape[3], volume.shape[4])
    totals = jnp.zeros(volume.shape, jnp.float32)
    for depth_off in range(3):
        for row_off in range(3):
            for col_off in range(3):
                window = padded[:, :, depth_off:depth_off + depth_len, row_off:row_off + row_count, col_off:col_off + col_count]
                totals = totals + jnp.einsum('og,bgdhw->bodhw', kernel[:, depth_off, row_off, col_off, :].astype(jnp.float32), window.astype(jnp.float32), precision=lax.Precision.HIGHEST)
    return totals

def attend_block(tokens, attn_weights):
    inverse = 1.0 / math.sqrt(tokens.shape[-1])
    floats = tokens.astype(jnp.float32)
    weights_f = attn_weights.astype(jnp.float32)
    queries = jnp.einsum('...dg,fg->...df', floats, weights_f[0], precision=lax.Precision.HIGHEST)
    key_rows = jnp.einsum('...dg,fg->...df', floats, weights_f[1], precision=lax.Precision.HIGHEST)
    values = jnp.einsum('...dg,fg->...df', floats, weights_f[2], precision=lax.Precision.HIGHEST).astype(jnp.bfloat16)
    scores = jnp.einsum('...df,...ef->...de', queries, key_rows, precision=lax.Precision.HIGHEST) * inverse
    chances = jax.nn.softmax(scores, axis=-1).astype(jnp.bfloat16)
    mixture = jnp.einsum('...de,...ef->...df', chances.astype(jnp.float32), values.astype(jnp.float32), precision=lax.Precision.HIGHEST)
    return floats + mixture

def summarize(attended, head):
    floats = attended.astype(jnp.float32)
    logits = lax.optimization_barrier(jnp.sum(floats * head, axis=-1))
    chances = jax.nn.softmax(logits, axis=-1)
    disp_values = jnp.arange(DISP, dtype=jnp.float32)
    disparity = lax.optimization_barrier(jnp.sum(chances * disp_values, axis=-1))
    spread = lax.optimization_barrier(jnp.sum((chances * (disp_values - disparity[..., None]))[..., None] * floats, axis=-2))
    return (disparity, spread)

def reference(left_features, right_features, stem_weights, conv_weights, attn_weights, head, target_disparity):
    right_pad = jnp.pad(right_features, ((0, 0), (0, 0), (0, 0), (DISP, 0)))
    cost_volume = correlate(left_features, right_pad, jnp.arange(DISP, dtype=jnp.int32), 0, W)
    lifted = lift(cost_volume, stem_weights)
    hidden = lifted
    for layer_no in range(LAYERS):
        totals = convolve(hidden, conv_weights[layer_no])
        if layer_no + 1 < LAYERS:
            hidden = jax.nn.relu(totals).astype(jnp.bfloat16)
        else:
            hidden = totals + lifted.astype(jnp.float32)
    tokens = hidden.transpose(0, 3, 4, 2, 1).reshape(BATCH * H, W, DISP, V)

    def per_row(row_tokens):
        return summarize(attend_block(row_tokens, attn_weights), head)
    disparity, spread = lax.map(per_row, tokens)
    disparity = disparity.reshape(BATCH, H, W)
    spread = spread.reshape(BATCH, H, W, V)
    residual = disparity - target_disparity
    magnitude = jnp.abs(residual)
    huber_terms = jnp.where(magnitude < 1.0, 0.5 * residual * residual, magnitude - 0.5)
    pixel_count = BATCH * H * W
    loss = jnp.sum(huber_terms) / pixel_count
    grad_disp = jnp.clip(residual, -1.0, 1.0) / pixel_count
    head_grad = lax.optimization_barrier(jnp.sum(grad_disp[..., None] * spread, axis=(0, 1, 2)))
    across = jnp.concatenate([disparity[:, :, 1:] - disparity[:, :, :-1], jnp.zeros((BATCH, H, 1), jnp.float32)], 2)
    downward = jnp.concatenate([disparity[:, 1:, :] - disparity[:, :-1, :], jnp.zeros((BATCH, 1, W), jnp.float32)], 1)
    inverse = 1.0 / jnp.sqrt(across * across + downward * downward + 1.0)
    normals = jnp.stack([-across * inverse, -downward * inverse, inverse])
    return (disparity, normals, loss, head_grad)
```

```python
import functools
import math

import jax
import jax.numpy as jnp
import numpy as np
from jax import lax
from jax.experimental import pallas as pl
from jax.experimental.pallas import tpu as pltpu
from jax.sharding import PartitionSpec as P

G = 8
V = 32
DISP = 104
SLABS = 7
PART = 16
ROWS_E = 17 * PART
COLS = 64
WIN_L = COLS + 4
WIN_R = COLS + 3 + DISP
BASE = COLS + 1
POSITION = (2, 3, 0, 1, 4, 5)
NT = (((1,), (1,)), ((), ()))
F32 = jnp.float32
BF16 = jnp.bfloat16


def iota(shape, dim):
    return lax.broadcasted_iota(jnp.int32, shape, dim)


def dot(a, b):
    return jnp.dot(a, b, preferred_element_type=F32)


def dot_nt(a, b):
    return lax.dot_general(a, b, NT, preferred_element_type=F32)


def one_hot(condition):
    return jnp.where(condition, 1.0, 0.0).astype(BF16)


def order_matrix():
    rows = iota((9 * PART, 128), 0)
    lanes = iota((9 * PART, 128), 1)
    wanted = (rows % PART) * SLABS + rows // PART - 1
    return one_hot((wanted == lanes) & (wanted >= 0) & (wanted < DISP))


def correlate(left, right, pick_left, pick_right, group_mask, out_ref, slot):
    spread = (dot_nt(pick_left, left) * group_mask).astype(BF16)
    turned = dot(right, pick_right).astype(BF16)
    out_ref[slot] = dot(spread, turned) * (1.0 / 28.0)


def volume_kernel(
    place,
    left,
    right,
    above,
    below,
    lift_w,
    w1,
    w2,
    query_w,
    value_w,
    head_col,
    target,
    out,
    corr,
    y,
    hidden,
    mask,
    x,
    att,
    logit,
    weight,
):
    disp_index, row_index, row_last = place[0], place[1], place[2]
    col0 = disp_index * COLS

    rows544 = iota((WIN_L * G, 256), 0)
    lanes544 = iota((WIN_L * G, 256), 1)
    ch = iota((WIN_L * G, 224), 1)
    grp = iota((WIN_L * G, 224), 0) % G
    group_mask = jnp.where((ch >= grp * 28) & (ch < grp * 28 + 28), 1.0, 0.0)
    u = iota((256, 256), 1)
    lane = iota((256, 256), 0)
    own_left = one_hot(lanes544 == rows544 // G + col0 - 2)
    own_right = one_hot((lane == col0 + BASE - u) & (u < WIN_R))
    halo_left = one_hot(lanes544 == rows544 // G)
    halo_right = one_hot((lane == WIN_L + WIN_R - 1 - u) & (u < WIN_R))
    for row in range(2):
        correlate(left[row], right[row], own_left, own_right, group_mask, corr, row)
        correlate(above[row], above[row], halo_left, halo_right, group_mask, corr, 2 + row)
        correlate(below[row], below[row], halo_left, halo_right, group_mask, corr, 4 + row)

    order = order_matrix()

    def lift_quad(quad, carry):
        pieces = []
        for wi in range(4):
            col = quad * 4 + wi
            back = WIN_L - 1 - col
            for slot in range(6):
                block = corr[slot, pl.ds(pl.multiple_of(col * G, G), G), :]
                pieces.append(pltpu.roll(block, lax.rem(256 - back, 256), 1)[:, :128])
        cost = jnp.concatenate(pieces, axis=0).astype(BF16)
        turned = dot_nt(order, cost).astype(BF16)
        lifted = dot(turned, lift_w[...]).astype(BF16)
        at = pl.ds(pl.multiple_of(quad * PART, PART), PART)
        for slab in range(9):
            piece = lifted[slab * PART : (slab + 1) * PART]
            y[slab, 0, at, :] = piece[:, :384]
            y[slab, 1, at, :] = piece[:, 384:]
        return carry

    lax.fori_loop(0, 17, lift_quad, 0)

    rows = iota((ROWS_E, 256), 0)
    lanes = iota((ROWS_E, 256), 1)
    wo, ro = lanes // 128, (lanes // 32) % 4
    inside = ((ro > 0) | (row_index > 0)) & ((ro < 3) | (row_index < row_last))
    first = (rows // PART == 0) & (wo == 0) & (disp_index == 0)
    last = (rows // PART == 16) & (wo == 1) & (disp_index == 3)
    even_ok = inside & ~first & ~last
    part = rows % PART
    for tail in range(2):
        deep = part < 15 - tail
        mask[tail, 0] = jnp.where(even_ok & deep, 1.0, 0.0)
        mask[tail, 1] = jnp.where(inside & deep, 1.0, 0.0)

    def conv1(slab, carry):
        tail = jnp.where(slab == SLABS, 1, 0)
        pieces = []
        for dq in range(3):
            pieces += [y[slab - 1 + dq, 0], y[slab - 1 + dq, 1]]
        even = jnp.maximum(dot(jnp.concatenate(pieces, axis=1), w1[...]), 0.0) * mask[tail, 0]
        hidden[slab, 0] = even.astype(BF16)
        pieces = []
        for dq in range(3):
            pieces += [y[slab - 1 + dq, 1, 0:256], y[slab - 1 + dq, 0, PART:ROWS_E]]
        odd = jnp.maximum(dot(jnp.concatenate(pieces, axis=1), w1[...]), 0.0) * mask[tail, 1, 0:256]
        hidden[slab, 1, 0:256] = odd.astype(BF16)
        return carry

    lax.fori_loop(1, SLABS + 1, conv1, 0)
    for parity, count in ((0, ROWS_E), (1, 256)):
        place_in = iota((count, 256), 0) % PART
        before = hidden[SLABS, parity, 0:count].astype(F32)
        before = jnp.where(place_in == 0, 0.0, pltpu.roll(before, 1, 0))
        hidden[0, parity, 0:count] = before.astype(BF16)
        after = hidden[1, parity, 0:count].astype(F32)
        after = jnp.where(place_in == PART - 1, 0.0, pltpu.roll(after, count - 1, 0))
        hidden[SLABS + 1, parity, 0:count] = after.astype(BF16)

    def conv2(slab, carry):
        pieces = []
        for dq in range(3):
            at = slab - 1 + dq
            pieces += [hidden[at, 0, 0:256], hidden[at, 1, 0:256], hidden[at, 0, PART:ROWS_E]]
        total = dot(jnp.concatenate(pieces, axis=1), w2[...])
        low = iota((256, 128), 1) < 64
        for half in range(2):
            source = y[slab, 1, 0:256] if half == 0 else y[slab, 0, PART:ROWS_E]
            own = jnp.where(low, source[:, 0:128].astype(F32), source[:, 128:256].astype(F32))
            x[half, slab - 1] = total[:, half * 128 : half * 128 + 128] + own
        return carry

    lax.fori_loop(1, SLABS + 1, conv2, 0)

    e_row = iota((SLABS * PART, 256), 0)
    e_valid = (e_row % PART) * SLABS + e_row // PART < DISP
    lane_px = iota((SLABS * PART, 128), 1) // 32

    def attend(quad, carry):
        at = pl.ds(pl.multiple_of(quad * PART, PART), PART)
        for half in range(2):
            tokens = jnp.concatenate([x[half, slab, at, :] for slab in range(SLABS)], axis=0)
            rounded = tokens.astype(BF16)
            queries = dot(rounded, query_w[...]).astype(BF16)
            values = dot_nt(value_w[...], rounded).astype(BF16)
            padded = jnp.concatenate([tokens, jnp.zeros((PART, 128), F32)], axis=0)
            turned = padded.T
            zeros = jnp.zeros((PART, 128), BF16)
            for pair in range(2):
                chosen = []
                for row in range(2):
                    px = pair * 2 + row
                    chosen += [jnp.where(lane_px == px, queries, jnp.zeros_like(queries)), zeros]
                scores = dot_nt(rounded, jnp.concatenate(chosen, axis=0))
                scores = jnp.where(e_valid, scores, -1e30)
                top = jnp.max(scores, axis=0, keepdims=True)
                grown = jnp.exp(scores - top)
                scale = 1.0 / jnp.sum(grown, axis=0, keepdims=True)
                chances = (grown * scale).astype(BF16)
                mixed = dot(values[pair * 64 : pair * 64 + 64], chances)
                for row in range(2):
                    px = pair * 2 + row
                    attended = (
                        turned[px * 32 : px * 32 + 32]
                        + mixed[row * 32 : row * 32 + 32, row * 128 : row * 128 + 128]
                    )
                    index = row * COLS + quad * 4 + half * 2 + pair
                    att[index] = attended
                    logit[pl.ds(index, 1), :] = jnp.sum(
                        attended * head_col[...], axis=0, keepdims=True
                    )
        return carry

    lax.fori_loop(0, 16, attend, 0)

    slot_lane = iota((128, 128), 1)
    depth = (slot_lane % PART) * SLABS + slot_lane // PART
    valid = (slot_lane < SLABS * PART) & (depth < DISP)
    depth_f = depth.astype(F32)
    logits = jnp.where(valid, logit[...], -1e30)
    grown = jnp.where(valid, jnp.exp(logits - jnp.max(logits, axis=1, keepdims=True)), 0.0)
    prob = grown / jnp.sum(grown, axis=1, keepdims=True)
    disparity = jnp.sum(prob * depth_f, axis=1, keepdims=True)
    disp_row = jnp.broadcast_to(disparity, (128, 128)).T[0:1]
    residual = disp_row - target[...]
    size = jnp.abs(residual)
    huber = jnp.where(size < 1.0, 0.5 * residual * residual, size - 0.5)
    pixels = 1.0 / ((row_last + 1) * (2 * 4 * COLS)).astype(F32)
    loss = jnp.sum(huber, axis=1, keepdims=True) * pixels
    slope = jnp.clip(residual, -1.0, 1.0) * pixels
    slope_col = jnp.broadcast_to(slope, (128, 128)).T
    weight[...] = slope_col * prob * (depth_f - disparity)

    def gather(block, total):
        for k in range(8):
            px = block * 8 + k
            total += att[px] * weight[pl.ds(px, 1), :]
        return total

    total = lax.fori_loop(0, 16, gather, jnp.zeros((V, 128), F32))
    padded = jnp.concatenate([total, jnp.zeros((128 - V, 128), F32)], axis=0)
    grads = jnp.sum(padded.T, axis=0, keepdims=True)
    out[0:1, :] = disp_row
    out[1:2, :] = jnp.where(iota((1, 128), 1) == V, loss, grads)


def toeplitz(kernel, cols_in, cols_out, rows_in, rows_out, positions):
    row_pick = np.zeros((3, rows_in, rows_out), np.float32)
    for slot in range(rows_in):
        for out_row in range(rows_out):
            off = positions[slot] - out_row
            if 0 <= off < 3:
                row_pick[off, slot, out_row] = 1
    col_pick = np.zeros((3, cols_in, cols_out), np.float32)
    for col in range(cols_in):
        for out_col in range(cols_out):
            if 0 <= col - out_col < 3:
                col_pick[col - out_col, col, out_col] = 1
    pick = np.einsum("jsr,kaw->jkaswr", row_pick, col_pick).reshape(9, -1)
    flat = kernel.transpose(1, 4, 0, 2, 3).reshape(3 * V * V, 9)
    chosen = dot(flat, jnp.asarray(pick, BF16)).astype(BF16)
    chosen = chosen.reshape(3, V, V, cols_in, rows_in, cols_out, rows_out)
    return chosen.transpose(0, 3, 4, 1, 5, 6, 2).reshape(3 * cols_in * rows_in * V, 256)


def lift_weights(stem):
    return jnp.kron(jnp.eye(24, dtype=BF16), stem.T)


def body(left, right, stem, conv, attn, head, target):
    disp_index = lax.axis_index("disp")
    row_index = lax.axis_index("rows")
    row_count = lax.axis_size("rows")
    left, right = left[0], right[0]
    col0 = disp_index * COLS
    pad_l = jnp.pad(left, ((0, 0), (0, 0), (2, 2)))
    pad_r = jnp.pad(right, ((0, 0), (0, 0), (DISP + 1, 2)))
    window = jnp.concatenate(
        [
            lax.dynamic_slice_in_dim(pad_l, col0, WIN_L, 2),
            lax.dynamic_slice_in_dim(pad_r, col0, WIN_R, 2),
            jnp.zeros((2, left.shape[1], 256 - WIN_L - WIN_R), BF16),
        ],
        axis=2,
    )
    down = [(r, r + 1) for r in range(row_count - 1)]
    up = [(r + 1, r) for r in range(row_count - 1)]
    above = lax.ppermute(window, "rows", down)
    below = lax.ppermute(window, "rows", up)
    w1 = toeplitz(conv[0], 4, 2, 6, 4, POSITION)
    w2 = toeplitz(conv[1], 6, 4, 4, 2, (0, 1, 2, 3))
    attn_f = attn.astype(F32)
    folded = jnp.dot(attn_f[0].T, attn_f[1], precision=lax.Precision.HIGHEST) / math.sqrt(V)
    eye = jnp.eye(4, dtype=BF16)
    query_w = jnp.kron(eye, folded.astype(BF16))
    value_w = jnp.kron(eye, attn[2])
    head_col = jnp.broadcast_to(head[:, None], (V, 128))
    own_target = lax.dynamic_slice_in_dim(target[0], col0, COLS, 1).reshape(1, 2 * COLS)
    place = jnp.stack([disp_index, row_index, jnp.int32(row_count - 1)]).astype(jnp.int32)
    vmem = pl.BlockSpec(memory_space=pltpu.VMEM)
    part = pl.pallas_call(
        volume_kernel,
        out_shape=jax.ShapeDtypeStruct((2, 128), F32),
        in_specs=[pl.BlockSpec(memory_space=pltpu.SMEM)] + [vmem] * 11,
        out_specs=vmem,
        scratch_shapes=[
            pltpu.VMEM((6, WIN_L * G, 256), F32),
            pltpu.VMEM((9, 2, ROWS_E, 384), BF16),
            pltpu.VMEM((9, 2, ROWS_E, 256), BF16),
            pltpu.VMEM((2, 2, ROWS_E, 256), F32),
            pltpu.VMEM((2, SLABS, 256, 128), F32),
            pltpu.VMEM((2 * COLS, V, 128), F32),
            pltpu.VMEM((2 * COLS, 128), F32),
            pltpu.VMEM((2 * COLS, 128), F32),
        ],
        compiler_params=pltpu.CompilerParams(vmem_limit_bytes=48 * 1024 * 1024),
        name="volume",
    )(place, left, right, above, below, lift_weights(stem), w1, w2, query_w, value_w, head_col, own_target)

    return finish(part, row_index, row_count)


def finish(part, row_index, row_count):
    sums = lax.psum(part[1], ("rows", "disp"))
    quarter = part[0].reshape(2, COLS)
    disparity = lax.all_gather(quarter, "disp", axis=1, tiled=True)
    up = [(r + 1, r) for r in range(row_count - 1)]
    following = lax.ppermute(disparity[:1], "rows", up)
    below_rows = jnp.concatenate([disparity[1:], following], 0)
    inside = (row_index * 2 + jnp.arange(2) < row_count * 2 - 1)[:, None]
    downward = jnp.where(inside, below_rows - disparity, 0.0)
    across = jnp.concatenate([disparity[:, 1:] - disparity[:, :-1], jnp.zeros((2, 1), F32)], 1)
    inverse = 1.0 / jnp.sqrt(across * across + downward * downward + 1.0)
    normals = jnp.stack([-across * inverse, -downward * inverse, inverse])
    return disparity[None], normals[:, None], sums[V], sums[:V]


def solution(mesh):
    rows4 = P(None, "rows", None, None)
    return jax.shard_map(
        body,
        mesh=mesh,
        in_specs=(rows4, rows4, P(), P(), P(), P(), P(None, "rows", None)),
        out_specs=(P(None, "rows", None), P(None, None, "rows", None), P(), P()),
        check_vma=False,
    )
```

```python
import math

import jax
import jax.numpy as jnp
from jax import lax
from jax.experimental import pallas as pl
from jax.experimental.pallas import tpu as pltpu
from jax.sharding import PartitionSpec as P

G = 8
V = 32
DISP = 104
SLABS = 7
PART = 16
ROWS_E = 17 * PART
COLS = 64
WIN_L = COLS + 4
WIN_R = COLS + 3 + DISP
BASE = COLS + 1
OWN, HALO = (2, 3), (0, 1, 4, 5)
K_OWN = 3 * 2 * 128
K_ALL = 3 * 2 * 384
NT = (((1,), (1,)), ((), ()))
TN = (((0,), (0,)), ((), ()))
F32 = jnp.float32
BF16 = jnp.bfloat16


def iota(shape, dim):
    return lax.broadcasted_iota(jnp.int32, shape, dim)


def dot(a, b):
    return jnp.dot(a, b, preferred_element_type=F32)


def dot_nt(a, b):
    return lax.dot_general(a, b, NT, preferred_element_type=F32)


def dot_tn(a, b):
    return lax.dot_general(a, b, TN, preferred_element_type=F32)


def one_hot(condition):
    return jnp.where(condition, 1.0, 0.0).astype(BF16)


def order_matrix():
    rows = iota((9 * PART, 128), 0)
    lanes = iota((9 * PART, 128), 1)
    wanted = (rows % PART) * SLABS + rows // PART - 1
    return one_hot((wanted == lanes) & (wanted >= 0) & (wanted < DISP))


def group_mask():
    ch = iota((WIN_L * G, 224), 1)
    grp = iota((WIN_L * G, 224), 0) % G
    return jnp.where((ch >= grp * 28) & (ch < grp * 28 + 28), 1.0, 0.0)


def correlate(left, right, pick_left, pick_right, mask):
    spread = (dot_nt(pick_left, left) * mask).astype(BF16)
    turned = dot(right, pick_right).astype(BF16)
    return dot(spread, turned) * (1.0 / 28.0)


def cost_of_quad(corr, quad, slots):
    pieces = []
    for wi in range(4):
        col = quad * 4 + wi
        shift = lax.rem(256 - (WIN_L - 1) + col, 256)
        for slot in range(slots):
            block = corr[slot, pl.ds(pl.multiple_of(col * G, G), G), :]
            pieces.append(pltpu.roll(block, shift, 1)[:, :128])
    return jnp.concatenate(pieces, axis=0).astype(BF16)


def pack_kernel(place, left, right, out):
    col0 = place[0] * COLS
    lane = iota((2 * 224, 256), 1)
    l_all = left[...].reshape(2 * 224, 256).astype(F32)
    r_all = right[...].reshape(2 * 224, 256).astype(F32)
    l_col, r_col = lane + col0 - 2, lane + col0 - (WIN_L + DISP + 1)
    l_all = pltpu.roll(l_all, lax.rem(258 - col0, 256), 1)
    r_all = pltpu.roll(r_all, lax.rem(256 + WIN_L + DISP + 1 - col0, 256), 1)
    l_all = jnp.where((l_col >= 0) & (l_col < 256), l_all, 0.0)
    r_all = jnp.where((r_col >= 0) & (r_col < 256) & (lane < WIN_L + WIN_R), r_all, 0.0)
    out[...] = jnp.where(lane < WIN_L, l_all, r_all).astype(BF16).reshape(2, 224, 256)


def block_diagonal(small, times):
    size = 32 * times
    up = one_hot(iota((size, 32), 0) % 32 == iota((size, 32), 1))
    across = one_hot(iota((32, size), 0) == iota((32, size), 1) % 32)
    tiled = dot(dot(up, small).astype(BF16), across)
    same = iota((size, size), 0) // 32 == iota((size, size), 1) // 32
    return jnp.where(same, tiled, 0.0).astype(BF16)


def place_taps(taps, group, depth, col, position, cols_out, rows_out):
    halves = []
    for half in range(2):
        total = jnp.zeros((V, 128), BF16)
        for spot in range(4):
            index = half * 4 + spot
            out_col, out_row = index // rows_out, index % rows_out
            j, k = position - out_row, col - out_col
            if 0 <= j < 3 and 0 <= k < 3:
                total = jnp.where(group == spot, taps[(depth * 3 + j) * 3 + k], total)
        halves.append(total)
    return jnp.concatenate(halves, axis=1)


def prep_kernel(
    place, left, right, conv, stem, attn, cost, w1, w2, lift_own, lift_halo, query_w, value_w, corr
):
    copies = one_hot(iota((V, 128), 0) == iota((V, 128), 1) % V)
    group = iota((V, 128), 1) // V
    for layer in range(2):
        taps = [dot_tn(conv[layer * 27 + tap], copies).astype(BF16) for tap in range(27)]
        for depth in range(3):
            if layer == 0:
                for a in range(2):
                    for wpar in range(2):
                        for start, width, spots in ((0, 128, OWN), (K_OWN, 256, HALO)):
                            for slot, position in enumerate(spots):
                                row = start + (depth * 2 + a) * width + (wpar * len(spots) + slot) * V
                                w1[row : row + V, :] = place_taps(
                                    taps, group, depth, a * 2 + wpar, position, 2, 4
                                )
            else:
                for col in range(6):
                    for slot in range(4):
                        row = ((depth * 6 + col) * 4 + slot) * V
                        w2[row : row + V, :] = place_taps(taps, group, depth, col, slot, 4, 2)
    for out, slots in ((lift_own, 2), (lift_halo, 4)):
        rows, cols = 4 * slots * G, 4 * slots * V
        up = one_hot(iota((rows, G), 0) % G == iota((rows, G), 1))
        across = one_hot(iota((V, cols), 0) == iota((V, cols), 1) % V)
        tiled = dot(dot(up, stem[...]).astype(BF16), across)
        same = iota((rows, cols), 0) // G == iota((rows, cols), 1) // V
        out[...] = jnp.where(same, tiled, 0.0).astype(BF16)
    folded = (dot_tn(attn[0], attn[1]) * (1.0 / math.sqrt(V))).astype(BF16)
    query_w[...] = block_diagonal(folded, 4)
    value_w[...] = block_diagonal(attn[2], 4)

    col0 = place[0] * COLS
    shape = (WIN_L * G, 256)
    pick_left = one_hot(iota(shape, 1) == iota(shape, 0) // G + col0 - 2)
    u = iota((256, 256), 1)
    pick_right = one_hot((iota((256, 256), 0) == col0 + BASE - u) & (u < WIN_R))
    mask = group_mask()
    for row in range(2):
        corr[row] = correlate(left[row], right[row], pick_left, pick_right, mask)

    def turn(quad, carry):
        cost[quad] = cost_of_quad(corr, quad, 2)
        return carry

    lax.fori_loop(0, 17, turn, 0)


def volume_kernel(
    place,
    above,
    below,
    cost,
    lift_own,
    lift_halo,
    w1,
    w2,
    query_w,
    value_w,
    head,
    target,
    out,
    corr,
    y_own,
    y_halo,
    hidden,
    mask,
    x,
    att,
    logit,
    weight,
):
    disp_index, row_index, row_last = place[0], place[1], place[2]
    col0 = disp_index * COLS

    shape = (WIN_L * G, 256)
    pick_left = one_hot(iota(shape, 1) == iota(shape, 0) // G)
    u = iota((256, 256), 1)
    pick_right = one_hot((iota((256, 256), 0) == WIN_L + WIN_R - 1 - u) & (u < WIN_R))
    channels = group_mask()
    for side, rows in enumerate((above, below)):
        there = row_index > 0 if side == 0 else row_index < row_last
        kept = channels * jnp.where(there, 1.0, 0.0)
        for row in range(2):
            corr[side * 2 + row] = correlate(rows[row], rows[row], pick_left, pick_right, kept)

    order = order_matrix()

    def lift_quad(quad, carry):
        costs = jnp.concatenate([cost[quad], cost_of_quad(corr, quad, 4)], axis=0)
        turned = dot_nt(order, costs).astype(BF16)
        own = dot(turned[:, :64], lift_own[...]).astype(BF16)
        halo = dot(turned[:, 64:], lift_halo[...]).astype(BF16)
        at = pl.ds(pl.multiple_of(quad * PART, PART), PART)
        for slab in range(9):
            part = slice(slab * PART, (slab + 1) * PART)
            for parity in range(2):
                y_own[slab, parity, at, :] = own[part, parity * 128 : parity * 128 + 128]
                y_halo[slab, parity, at, :] = halo[part, parity * 256 : parity * 256 + 256]
        return carry

    lax.fori_loop(0, 17, lift_quad, 0)

    rows = iota((ROWS_E, 256), 0)
    lanes = iota((ROWS_E, 256), 1)
    wo, ro = lanes // 128, (lanes // 32) % 4
    inside = ((ro > 0) | (row_index > 0)) & ((ro < 3) | (row_index < row_last))
    first = (rows // PART == 0) & (wo == 0) & (disp_index == 0)
    last = (rows // PART == 16) & (wo == 1) & (disp_index == 3)
    even_ok = inside & ~first & ~last
    part = rows % PART
    for tail in range(2):
        deep = part < 15 - tail
        mask[tail, 0] = jnp.where(even_ok & deep, 1.0, 0.0)
        mask[tail, 1] = jnp.where(inside & deep, 1.0, 0.0)

    def conv1(slab, carry):
        tail = jnp.where(slab == SLABS, 1, 0)
        for parity in range(2):
            if parity == 0:
                spans = ((0, 0, ROWS_E), (1, 0, ROWS_E))
            else:
                spans = ((1, 0, 256), (0, PART, ROWS_E))
            pieces = []
            for y in (y_own, y_halo):
                for dq in range(3):
                    pieces += [y[slab - 1 + dq, at, low:high] for at, low, high in spans]
            count = spans[0][2]
            total = dot(jnp.concatenate(pieces, axis=1), w1[...])
            total = jnp.maximum(total, 0.0) * mask[tail, parity, 0:count]
            hidden[slab, parity, 0:count] = total.astype(BF16)
        return carry

    lax.fori_loop(1, SLABS + 1, conv1, 0)
    for parity, count in ((0, ROWS_E), (1, 256)):
        place_in = iota((count, 256), 0) % PART
        before = hidden[SLABS, parity, 0:count].astype(F32)
        before = jnp.where(place_in == 0, 0.0, pltpu.roll(before, 1, 0))
        hidden[0, parity, 0:count] = before.astype(BF16)
        after = hidden[1, parity, 0:count].astype(F32)
        after = jnp.where(place_in == PART - 1, 0.0, pltpu.roll(after, count - 1, 0))
        hidden[SLABS + 1, parity, 0:count] = after.astype(BF16)

    def conv2(slab, carry):
        pieces = []
        for dq in range(3):
            at = slab - 1 + dq
            pieces += [hidden[at, 0, 0:256], hidden[at, 1, 0:256], hidden[at, 0, PART:ROWS_E]]
        total = dot(jnp.concatenate(pieces, axis=1), w2[...])
        x[0, slab - 1] = total[:, :128] + y_own[slab, 1, 0:256].astype(F32)
        x[1, slab - 1] = total[:, 128:] + y_own[slab, 0, PART:ROWS_E].astype(F32)
        return carry

    lax.fori_loop(1, SLABS + 1, conv2, 0)

    e_row = iota((SLABS * PART, 256), 0)
    e_valid = (e_row % PART) * SLABS + e_row // PART < DISP
    lane_px = iota((SLABS * PART, 128), 1) // 32
    head_col = jnp.zeros((V, 128), F32)
    for v in range(V):
        head_col = jnp.where(iota((V, 128), 0) == v, head[v], head_col)

    def attend(quad, carry):
        at = pl.ds(pl.multiple_of(quad * PART, PART), PART)
        for half in range(2):
            tokens = jnp.concatenate([x[half, slab, at, :] for slab in range(SLABS)], axis=0)
            rounded = tokens.astype(BF16)
            queries = dot(rounded, query_w[...]).astype(BF16)
            values = dot_nt(value_w[...], rounded).astype(BF16)
            padded = jnp.concatenate([tokens, jnp.zeros((PART, 128), F32)], axis=0)
            turned = padded.T
            zeros = jnp.zeros((PART, 128), BF16)
            for pair in range(2):
                chosen = []
                for row in range(2):
                    px = pair * 2 + row
                    chosen += [jnp.where(lane_px == px, queries, jnp.zeros_like(queries)), zeros]
                scores = dot_nt(rounded, jnp.concatenate(chosen, axis=0))
                scores = jnp.where(e_valid, scores, -1e30)
                top = jnp.max(scores, axis=0, keepdims=True)
                grown = jnp.exp(scores - top)
                scale = 1.0 / jnp.sum(grown, axis=0, keepdims=True)
                chances = (grown * scale).astype(BF16)
                mixed = dot(values[pair * 64 : pair * 64 + 64], chances)
                for row in range(2):
                    px = pair * 2 + row
                    attended = (
                        turned[px * 32 : px * 32 + 32]
                        + mixed[row * 32 : row * 32 + 32, row * 128 : row * 128 + 128]
                    )
                    index = row * COLS + quad * 4 + half * 2 + pair
                    att[index] = attended
                    logit[pl.ds(index, 1), :] = jnp.sum(
                        attended * head_col, axis=0, keepdims=True
                    )
        return carry

    lax.fori_loop(0, 16, attend, 0)

    slot_lane = iota((128, 128), 1)
    depth = (slot_lane % PART) * SLABS + slot_lane // PART
    valid = (slot_lane < SLABS * PART) & (depth < DISP)
    depth_f = depth.astype(F32)
    logits = jnp.where(valid, logit[...], -1e30)
    grown = jnp.where(valid, jnp.exp(logits - jnp.max(logits, axis=1, keepdims=True)), 0.0)
    prob = grown / jnp.sum(grown, axis=1, keepdims=True)
    disparity = jnp.sum(prob * depth_f, axis=1, keepdims=True)
    disp_row = jnp.broadcast_to(disparity, (128, 128)).T[0:1]
    turned = [pltpu.roll(target[...], lax.rem(256 + row * COLS - col0, 256), 1) for row in range(2)]
    lane_row = iota((1, 128), 1)
    wanted = jnp.where(lane_row < COLS, turned[0][0:1, :128], turned[1][1:2, :128])
    residual = disp_row - wanted
    size = jnp.abs(residual)
    huber = jnp.where(size < 1.0, 0.5 * residual * residual, size - 0.5)
    pixels = 1.0 / ((row_last + 1) * (2 * 4 * COLS)).astype(F32)
    loss = jnp.sum(huber, axis=1, keepdims=True) * pixels
    slope = jnp.clip(residual, -1.0, 1.0) * pixels
    slope_col = jnp.broadcast_to(slope, (128, 128)).T
    weight[...] = slope_col * prob * (depth_f - disparity)

    def gather(block, total):
        for k in range(8):
            px = block * 8 + k
            total += att[px] * weight[pl.ds(px, 1), :]
        return total

    total = lax.fori_loop(0, 16, gather, jnp.zeros((V, 128), F32))
    padded = jnp.concatenate([total, jnp.zeros((128 - V, 128), F32)], axis=0)
    grads = jnp.sum(padded.T, axis=0, keepdims=True)
    sums = jnp.where(lane_row == V, loss, grads)
    out[...] = jnp.broadcast_to(jnp.concatenate([disp_row, sums], axis=0)[None], (128, 2, 128))


def finish_kernel(place, everyone, disparity, normals, loss, head_grad):
    row_index, row_last = place[1], place[2]
    sums = jnp.sum(everyone[...], axis=0)[1:2]
    head_grad[...] = sums[:, :V]
    loss[0, 0] = jnp.sum(jnp.where(iota((1, 128), 1) == V, sums, 0.0))
    low = iota((8, 128), 1) < COLS
    bands = []
    for band in range(2):
        start = jnp.minimum(row_index + band, row_last) * 4
        lines = [
            jnp.broadcast_to(everyone[start + k][0:1], (8, 128)) for k in range(4)
        ]
        swapped = [pltpu.roll(line, COLS, 1) for line in lines]
        tops = [jnp.where(low, lines[k], swapped[k + 1]) for k in (0, 2)]
        bottoms = [jnp.where(low, swapped[k], lines[k + 1]) for k in (0, 2)]
        bands += [jnp.concatenate(tops, axis=1), jnp.concatenate(bottoms, axis=1)]
    top, bottom, follow = bands[0], bands[1], bands[2]
    step = jnp.where(row_index < row_last, 1.0, 0.0)
    lane = iota((8, 256), 1)
    for row, (here, below, scale) in enumerate(((top, bottom, 1.0), (bottom, follow, step))):
        downward = (below - here) * scale
        across = jnp.where(lane < 255, pltpu.roll(here, 255, 1) - here, 0.0)
        inverse = 1.0 / jnp.sqrt(across * across + downward * downward + 1.0)
        disparity[0, row : row + 1, :] = here[0:1]
        normals[0, 0, row : row + 1, :] = (-across * inverse)[0:1]
        normals[1, 0, row : row + 1, :] = (-downward * inverse)[0:1]
        normals[2, 0, row : row + 1, :] = inverse[0:1]


VMEM_SPEC = pl.BlockSpec(memory_space=pltpu.VMEM)
SMEM_SPEC = pl.BlockSpec(memory_space=pltpu.SMEM)
PARAMS = pltpu.CompilerParams(vmem_limit_bytes=48 * 1024 * 1024)


def arr(dtype, *shape):
    return jax.ShapeDtypeStruct(shape, dtype)


def body(left, right, stem, conv, attn, head, target):
    disp_index = lax.axis_index("disp")
    row_index = lax.axis_index("rows")
    row_count = lax.axis_size("rows")
    left, right = left[0], right[0]
    place = jnp.stack([disp_index, row_index, jnp.int32(row_count - 1)]).astype(jnp.int32)
    window = pl.pallas_call(
        pack_kernel,
        out_shape=arr(BF16, 2, 224, 256),
        in_specs=[SMEM_SPEC, VMEM_SPEC, VMEM_SPEC],
        out_specs=VMEM_SPEC,
        compiler_params=PARAMS,
        name="pack",
    )(place, left, right)
    down = [(r, (r + 1) % row_count) for r in range(row_count)]
    up = [((r + 1) % row_count, r) for r in range(row_count)]
    above = lax.ppermute(window, "rows", down)
    below = lax.ppermute(window, "rows", up)
    cost, w1, w2, lift_own, lift_halo, query_w, value_w = pl.pallas_call(
        prep_kernel,
        out_shape=(
            arr(BF16, 17, 64, 128),
            arr(BF16, K_ALL, 256),
            arr(BF16, K_ALL, 256),
            arr(BF16, 64, 256),
            arr(BF16, 128, 512),
            arr(BF16, 128, 128),
            arr(BF16, 128, 128),
        ),
        in_specs=[SMEM_SPEC] + [VMEM_SPEC] * 5,
        out_specs=(VMEM_SPEC,) * 7,
        scratch_shapes=[pltpu.VMEM((2, WIN_L * G, 256), F32)],
        compiler_params=PARAMS,
        cost_estimate=pl.CostEstimate(flops=6 * 10**9, bytes_accessed=4 * 10**6, transcendentals=0),
        name="prep",
    )(place, left, right, conv.transpose(0, 2, 3, 4, 1, 5).reshape(54, V, V), stem.T, attn)
    shares = pl.pallas_call(
        volume_kernel,
        out_shape=arr(F32, 128, 2, 128),
        in_specs=[SMEM_SPEC] + [VMEM_SPEC] * 9 + [SMEM_SPEC, VMEM_SPEC],
        out_specs=VMEM_SPEC,
        scratch_shapes=[
            pltpu.VMEM((4, WIN_L * G, 256), F32),
            pltpu.VMEM((9, 2, ROWS_E, 128), BF16),
            pltpu.VMEM((9, 2, ROWS_E, 256), BF16),
            pltpu.VMEM((9, 2, ROWS_E, 256), BF16),
            pltpu.VMEM((2, 2, ROWS_E, 256), F32),
            pltpu.VMEM((2, SLABS, 256, 128), F32),
            pltpu.VMEM((2 * COLS, V, 128), F32),
            pltpu.VMEM((2 * COLS, 128), F32),
            pltpu.VMEM((2 * COLS, 128), F32),
        ],
        compiler_params=PARAMS,
        name="volume",
    )(place, above, below, cost, lift_own, lift_halo, w1, w2, query_w, value_w, head, target[0])
    everyone = lax.all_to_all(shares, ("rows", "disp"), 0, 0, tiled=True)
    disparity, normals, loss, head_grad = pl.pallas_call(
        finish_kernel,
        out_shape=(arr(F32, 1, 2, 256), arr(F32, 3, 1, 2, 256), arr(F32, 1, 1), arr(F32, 1, V)),
        in_specs=[SMEM_SPEC, VMEM_SPEC],
        out_specs=(VMEM_SPEC, VMEM_SPEC, SMEM_SPEC, VMEM_SPEC),
        compiler_params=PARAMS,
        name="finish",
    )(place, everyone)
    return disparity, normals, loss.reshape(()), head_grad.reshape(V)


def solution(mesh):
    rows4 = P(None, "rows", None, None)
    return jax.shard_map(
        body,
        mesh=mesh,
        in_specs=(rows4, rows4, P(), P(), P(), P(), P(None, "rows", None)),
        out_specs=(P(None, "rows", None), P(None, None, "rows", None), P(), P()),
        check_vma=False,
    )
```

```python
import math

import jax
import jax.numpy as jnp
from jax import lax
from jax.experimental import pallas as pl
from jax.experimental.pallas import tpu as pltpu
from jax.sharding import PartitionSpec as P

G = 8
V = 32
DISP = 104
SLABS = 7
PART = 16
ROWS_E = 17 * PART
COLS = 64
WIN_L = COLS + 4
WIN_R = COLS + 3 + DISP
BASE = COLS + 1
OWN, HALO = (2, 3), (0, 1, 4, 5)
K_OWN = 3 * 2 * 128
K_ALL = 3 * 2 * 384
NT = (((1,), (1,)), ((), ()))
TN = (((0,), (0,)), ((), ()))
F32 = jnp.float32
BF16 = jnp.bfloat16


def iota(shape, dim):
    return lax.broadcasted_iota(jnp.int32, shape, dim)


def dot(a, b):
    return jnp.dot(a, b, preferred_element_type=F32)


def dot_nt(a, b):
    return lax.dot_general(a, b, NT, preferred_element_type=F32)


def dot_tn(a, b):
    return lax.dot_general(a, b, TN, preferred_element_type=F32)


def one_hot(condition):
    return jnp.where(condition, 1.0, 0.0).astype(BF16)


def order_matrix():
    rows = iota((9 * PART, 128), 0)
    lanes = iota((9 * PART, 128), 1)
    wanted = (rows % PART) * SLABS + rows // PART - 1
    return one_hot((wanted == lanes) & (wanted >= 0) & (wanted < DISP))


def group_mask():
    ch = iota((WIN_L * G, 224), 1)
    grp = iota((WIN_L * G, 224), 0) % G
    return jnp.where((ch >= grp * 28) & (ch < grp * 28 + 28), 1.0, 0.0)


def correlate(left, right, pick_left, pick_right, mask):
    spread = (dot_nt(pick_left, left) * mask).astype(BF16)
    turned = dot(right, pick_right).astype(BF16)
    return dot(spread, turned) * (1.0 / 28.0)


def cost_of_quad(corr, quad, slots):
    pieces = []
    for wi in range(4):
        col = quad * 4 + wi
        shift = lax.rem(256 - (WIN_L - 1) + col, 256)
        for slot in range(slots):
            block = corr[slot, pl.ds(pl.multiple_of(col * G, G), G), :]
            pieces.append(pltpu.roll(block, shift, 1)[:, :128])
    return jnp.concatenate(pieces, axis=0)


def pack_kernel(place, left, right, out):
    col0 = place[0] * COLS
    lane = iota((2 * 224, 256), 1)
    l_all = left[...].reshape(2 * 224, 256).astype(F32)
    r_all = right[...].reshape(2 * 224, 256).astype(F32)
    l_col, r_col = lane + col0 - 2, lane + col0 - (WIN_L + DISP + 1)
    l_all = pltpu.roll(l_all, lax.rem(258 - col0, 256), 1)
    r_all = pltpu.roll(r_all, lax.rem(256 + WIN_L + DISP + 1 - col0, 256), 1)
    l_all = jnp.where((l_col >= 0) & (l_col < 256), l_all, 0.0)
    r_all = jnp.where((r_col >= 0) & (r_col < 256) & (lane < WIN_L + WIN_R), r_all, 0.0)
    out[...] = jnp.where(lane < WIN_L, l_all, r_all).astype(BF16).reshape(2, 224, 256)


def block_diagonal(small, times):
    size = 32 * times
    up = one_hot(iota((size, 32), 0) % 32 == iota((size, 32), 1))
    across = one_hot(iota((32, size), 0) == iota((32, size), 1) % 32)
    tiled = dot(dot(up, small).astype(BF16), across)
    same = iota((size, size), 0) // 32 == iota((size, size), 1) // 32
    return jnp.where(same, tiled, 0.0).astype(BF16)


def place_taps(taps, group, depth, col, position, cols_out, rows_out):
    halves = []
    for half in range(2):
        total = jnp.zeros((V, 128), BF16)
        for spot in range(4):
            index = half * 4 + spot
            out_col, out_row = index // rows_out, index % rows_out
            j, k = position - out_row, col - out_col
            if 0 <= j < 3 and 0 <= k < 3:
                total = jnp.where(group == spot, taps[(depth * 3 + j) * 3 + k], total)
        halves.append(total)
    return jnp.concatenate(halves, axis=1)


def prep_kernel(
    place, left, right, conv, stem, attn, cost, w1, w2, lift_own, lift_halo, derive_w, corr
):
    copies = one_hot(iota((V, 128), 0) == iota((V, 128), 1) % V)
    group = iota((V, 128), 1) // V
    for layer in range(2):
        taps = [dot_tn(conv[layer * 27 + tap], copies).astype(BF16) for tap in range(27)]
        for depth in range(3):
            if layer == 0:
                for a in range(2):
                    for wpar in range(2):
                        for start, width, spots in ((0, 128, OWN), (K_OWN, 256, HALO)):
                            for slot, position in enumerate(spots):
                                row = start + (depth * 2 + a) * width + (wpar * len(spots) + slot) * V
                                w1[row : row + V, :] = place_taps(
                                    taps, group, depth, a * 2 + wpar, position, 2, 4
                                )
            else:
                for col in range(6):
                    for slot in range(4):
                        row = ((depth * 6 + col) * 4 + slot) * V
                        w2[row : row + V, :] = place_taps(taps, group, depth, col, slot, 4, 2)
    for out, slots in ((lift_own, 2), (lift_halo, 4)):
        rows, cols = 128, 4 * slots * V
        up = one_hot(iota((rows, G), 0) % G == iota((rows, G), 1))
        across = one_hot(iota((V, cols), 0) == iota((V, cols), 1) % V)
        tiled = dot(dot(up, stem[...]).astype(BF16), across)
        same = iota((rows, cols), 0) // G == iota((rows, cols), 1) // V
        out[...] = jnp.where(same, tiled, 0.0).astype(BF16)
    folded = (dot_tn(attn[1], attn[0]) * (1.0 / math.sqrt(V))).astype(BF16)
    derive_w[0:128, :] = block_diagonal(folded, 4)
    derive_w[128:256, :] = block_diagonal(attn[2], 4)

    col0 = place[0] * COLS
    shape = (WIN_L * G, 256)
    pick_left = one_hot(iota(shape, 1) == iota(shape, 0) // G + col0 - 2)
    u = iota((256, 256), 1)
    pick_right = one_hot((iota((256, 256), 0) == col0 + BASE - u) & (u < WIN_R))
    mask = group_mask()
    for row in range(2):
        corr[row] = correlate(left[row], right[row], pick_left, pick_right, mask)

    def turn(quad, carry):
        own = jnp.concatenate([cost_of_quad(corr, quad, 2), jnp.zeros((64, 128), F32)], axis=0)
        cost[quad] = own.T.astype(BF16)
        return carry

    lax.fori_loop(0, 17, turn, 0, unroll=17)


def volume_kernel(
    place,
    above,
    below,
    cost,
    lift_own,
    lift_halo,
    w1,
    w2,
    derive_w,
    head,
    target,
    out,
    corr,
    y_own,
    y_halo,
    hidden,
    mask,
    x,
    att,
    logit,
    weight,
):
    disp_index, row_index, row_last = place[0], place[1], place[2]
    col0 = disp_index * COLS

    shape = (WIN_L * G, 256)
    pick_left = one_hot(iota(shape, 1) == iota(shape, 0) // G)
    u = iota((256, 256), 1)
    pick_right = one_hot((iota((256, 256), 0) == WIN_L + WIN_R - 1 - u) & (u < WIN_R))
    channels = group_mask()
    for side, rows in enumerate((above, below)):
        there = row_index > 0 if side == 0 else row_index < row_last
        kept = channels * jnp.where(there, 1.0, 0.0)
        for row in range(2):
            corr[side * 2 + row] = correlate(rows[row], rows[row], pick_left, pick_right, kept)

    order = order_matrix()

    def lift_quad(quad, carry):
        costs = dot(order, cost_of_quad(corr, quad, 4).T.astype(BF16)).astype(BF16)
        own = dot(dot(order, cost[quad]).astype(BF16), lift_own[...]).astype(BF16)
        halo = dot(costs, lift_halo[...]).astype(BF16)
        at = pl.ds(pl.multiple_of(quad * PART, PART), PART)
        for slab in range(9):
            part = slice(slab * PART, (slab + 1) * PART)
            for parity in range(2):
                y_own[slab, parity, at, :] = own[part, parity * 128 : parity * 128 + 128]
                y_halo[slab, parity, at, :] = halo[part, parity * 256 : parity * 256 + 256]
        return carry

    lax.fori_loop(0, 17, lift_quad, 0, unroll=17)

    rows = iota((ROWS_E, 256), 0)
    lanes = iota((ROWS_E, 256), 1)
    wo, ro = lanes // 128, (lanes // 32) % 4
    inside = ((ro > 0) | (row_index > 0)) & ((ro < 3) | (row_index < row_last))
    first = (rows // PART == 0) & (wo == 0) & (disp_index == 0)
    last = (rows // PART == 16) & (wo == 1) & (disp_index == 3)
    even_ok = inside & ~first & ~last
    part = rows % PART
    for tail in range(2):
        deep = part < 15 - tail
        mask[tail, 0] = jnp.where(even_ok & deep, 1.0, 0.0)
        mask[tail, 1] = jnp.where(inside & deep, 1.0, 0.0)

    def conv1(slab, carry):
        tail = jnp.where(slab == SLABS, 1, 0)
        for parity in range(2):
            if parity == 0:
                spans = ((0, 0, ROWS_E), (1, 0, ROWS_E))
            else:
                spans = ((1, 0, 256), (0, PART, ROWS_E))
            pieces = []
            for y in (y_own, y_halo):
                for dq in range(3):
                    pieces += [y[slab - 1 + dq, at, low:high] for at, low, high in spans]
            count = spans[0][2]
            total = dot(jnp.concatenate(pieces, axis=1), w1[...])
            total = jnp.maximum(total, 0.0) * mask[tail, parity, 0:count]
            hidden[slab, parity, 0:count] = total.astype(BF16)
        return carry

    lax.fori_loop(1, SLABS + 1, conv1, 0, unroll=7)
    for parity, count in ((0, ROWS_E), (1, 256)):
        place_in = iota((count, 256), 0) % PART
        before = hidden[SLABS, parity, 0:count].astype(F32)
        before = jnp.where(place_in == 0, 0.0, pltpu.roll(before, 1, 0))
        hidden[0, parity, 0:count] = before.astype(BF16)
        after = hidden[1, parity, 0:count].astype(F32)
        after = jnp.where(place_in == PART - 1, 0.0, pltpu.roll(after, count - 1, 0))
        hidden[SLABS + 1, parity, 0:count] = after.astype(BF16)

    def conv2(slab, carry):
        pieces = []
        for dq in range(3):
            at = slab - 1 + dq
            pieces += [hidden[at, 0, 0:256], hidden[at, 1, 0:256], hidden[at, 0, PART:ROWS_E]]
        total = dot(jnp.concatenate(pieces, axis=1), w2[...])
        x[0, slab - 1] = total[:, :128] + y_own[slab, 1, 0:256].astype(F32)
        x[1, slab - 1] = total[:, 128:] + y_own[slab, 0, PART:ROWS_E].astype(F32)
        return carry

    lax.fori_loop(1, SLABS + 1, conv2, 0, unroll=7)

    e_row = iota((SLABS * PART, 256), 0)
    e_valid = (e_row % PART) * SLABS + e_row // PART < DISP
    head_col = jnp.zeros((V, 128), F32)
    for v in range(V):
        head_col = jnp.where(iota((V, 128), 0) == v, head[v], head_col)

    def attend(quad, carry):
        at = pl.ds(pl.multiple_of(quad * PART, PART), PART)
        for half in range(2):
            tokens = jnp.concatenate([x[half, slab, at, :] for slab in range(SLABS)], axis=0)
            rounded = tokens.astype(BF16)
            padded = jnp.concatenate([tokens, jnp.zeros((PART, 128), F32)], axis=0)
            turned = padded.T
            derived = dot(derive_w[...], turned.astype(BF16)).astype(BF16)
            queries, values = derived[:128], derived[128:]
            for pair in range(2):
                chosen = []
                for row in range(2):
                    at_px = slice((pair * 2 + row) * 32, (pair * 2 + row) * 32 + 32)
                    above_px = jnp.zeros((at_px.start, 128), BF16)
                    below_px = jnp.zeros((128 - at_px.stop, 128), BF16)
                    pieces = [above_px, queries[at_px], below_px]
                    chosen.append(jnp.concatenate([k for k in pieces if k.shape[0]], axis=0))
                scores = dot(rounded, jnp.concatenate(chosen, axis=1))
                scores = jnp.where(e_valid, scores, -1e30)
                top = jnp.max(scores, axis=0, keepdims=True)
                grown = jnp.exp(scores - top)
                scale = 1.0 / jnp.sum(grown, axis=0, keepdims=True)
                chances = (grown * scale).astype(BF16)
                chances = jnp.concatenate([chances, jnp.zeros((PART, 256), BF16)], axis=0)
                mixed = dot(values[pair * 64 : pair * 64 + 64], chances)
                for row in range(2):
                    px = pair * 2 + row
                    attended = (
                        turned[px * 32 : px * 32 + 32]
                        + mixed[row * 32 : row * 32 + 32, row * 128 : row * 128 + 128]
                    )
                    index = row * COLS + quad * 4 + half * 2 + pair
                    att[index] = attended
                    logit[pl.ds(index, 1), :] = jnp.sum(
                        attended * head_col, axis=0, keepdims=True
                    )
        return carry

    lax.fori_loop(0, 16, attend, 0, unroll=8)

    slot_lane = iota((128, 128), 1)
    depth = (slot_lane % PART) * SLABS + slot_lane // PART
    valid = (slot_lane < SLABS * PART) & (depth < DISP)
    depth_f = depth.astype(F32)
    logits = jnp.where(valid, logit[...], -1e30)
    grown = jnp.where(valid, jnp.exp(logits - jnp.max(logits, axis=1, keepdims=True)), 0.0)
    prob = grown / jnp.sum(grown, axis=1, keepdims=True)
    disparity = jnp.sum(prob * depth_f, axis=1, keepdims=True)
    disp_row = jnp.broadcast_to(disparity, (128, 128)).T[0:1]
    turned = [pltpu.roll(target[...], lax.rem(256 + row * COLS - col0, 256), 1) for row in range(2)]
    lane_row = iota((1, 128), 1)
    wanted = jnp.where(lane_row < COLS, turned[0][0:1, :128], turned[1][1:2, :128])
    residual = disp_row - wanted
    size = jnp.abs(residual)
    huber = jnp.where(size < 1.0, 0.5 * residual * residual, size - 0.5)
    pixels = 1.0 / ((row_last + 1) * (2 * 4 * COLS)).astype(F32)
    loss = jnp.sum(huber, axis=1, keepdims=True) * pixels
    slope = jnp.clip(residual, -1.0, 1.0) * pixels
    slope_col = jnp.broadcast_to(slope, (128, 128)).T
    weight[...] = slope_col * prob * (depth_f - disparity)

    def gather(block, total):
        for k in range(8):
            px = block * 8 + k
            total += att[px] * weight[pl.ds(px, 1), :]
        return total

    total = lax.fori_loop(0, 16, gather, jnp.zeros((V, 128), F32))
    padded = jnp.concatenate([total, jnp.zeros((128 - V, 128), F32)], axis=0)
    grads = jnp.sum(padded.T, axis=0, keepdims=True)
    sums = jnp.where(lane_row == V, loss, grads)
    out[...] = jnp.broadcast_to(jnp.concatenate([disp_row, sums], axis=0)[None], (128, 2, 128))


def finish_kernel(place, everyone, disparity, normals, loss, head_grad):
    row_index, row_last = place[1], place[2]
    sums = jnp.sum(everyone[...], axis=0)[1:2]
    head_grad[...] = sums[:, :V]
    loss[0, 0] = jnp.sum(jnp.where(iota((1, 128), 1) == V, sums, 0.0))
    low = iota((8, 128), 1) < COLS
    bands = []
    for band in range(2):
        start = jnp.minimum(row_index + band, row_last) * 4
        lines = [
            jnp.broadcast_to(everyone[start + k][0:1], (8, 128)) for k in range(4)
        ]
        swapped = [pltpu.roll(line, COLS, 1) for line in lines]
        tops = [jnp.where(low, lines[k], swapped[k + 1]) for k in (0, 2)]
        bottoms = [jnp.where(low, swapped[k], lines[k + 1]) for k in (0, 2)]
        bands += [jnp.concatenate(tops, axis=1), jnp.concatenate(bottoms, axis=1)]
    top, bottom, follow = bands[0], bands[1], bands[2]
    step = jnp.where(row_index < row_last, 1.0, 0.0)
    lane = iota((8, 256), 1)
    for row, (here, below, scale) in enumerate(((top, bottom, 1.0), (bottom, follow, step))):
        downward = (below - here) * scale
        across = jnp.where(lane < 255, pltpu.roll(here, 255, 1) - here, 0.0)
        inverse = 1.0 / jnp.sqrt(across * across + downward * downward + 1.0)
        disparity[0, row : row + 1, :] = here[0:1]
        normals[0, 0, row : row + 1, :] = (-across * inverse)[0:1]
        normals[1, 0, row : row + 1, :] = (-downward * inverse)[0:1]
        normals[2, 0, row : row + 1, :] = inverse[0:1]


VMEM_SPEC = pl.BlockSpec(memory_space=pltpu.VMEM)
SMEM_SPEC = pl.BlockSpec(memory_space=pltpu.SMEM)
PARAMS = pltpu.CompilerParams(vmem_limit_bytes=48 * 1024 * 1024)


def arr(dtype, *shape):
    return jax.ShapeDtypeStruct(shape, dtype)


def body(left, right, stem, conv, attn, head, target):
    disp_index = lax.axis_index("disp")
    row_index = lax.axis_index("rows")
    row_count = lax.axis_size("rows")
    left, right = left[0], right[0]
    place = jnp.stack([disp_index, row_index, jnp.int32(row_count - 1)]).astype(jnp.int32)
    window = pl.pallas_call(
        pack_kernel,
        out_shape=arr(BF16, 2, 224, 256),
        in_specs=[SMEM_SPEC, VMEM_SPEC, VMEM_SPEC],
        out_specs=VMEM_SPEC,
        compiler_params=PARAMS,
        name="pack",
    )(place, left, right)
    down = [(r, (r + 1) % row_count) for r in range(row_count)]
    up = [((r + 1) % row_count, r) for r in range(row_count)]
    above = lax.ppermute(window, "rows", down)
    below = lax.ppermute(window, "rows", up)
    cost, w1, w2, lift_own, lift_halo, derive_w = pl.pallas_call(
        prep_kernel,
        out_shape=(
            arr(BF16, 17, 128, 128),
            arr(BF16, K_ALL, 256),
            arr(BF16, K_ALL, 256),
            arr(BF16, 128, 256),
            arr(BF16, 128, 512),
            arr(BF16, 256, 128),
        ),
        in_specs=[SMEM_SPEC] + [VMEM_SPEC] * 5,
        out_specs=(VMEM_SPEC,) * 6,
        scratch_shapes=[pltpu.VMEM((2, WIN_L * G, 256), F32)],
        compiler_params=PARAMS,
        cost_estimate=pl.CostEstimate(flops=6 * 10**9, bytes_accessed=4 * 10**6, transcendentals=0),
        name="prep",
    )(place, left, right, conv.transpose(0, 2, 3, 4, 1, 5).reshape(54, V, V), stem.T, attn)
    shares = pl.pallas_call(
        volume_kernel,
        out_shape=arr(F32, 128, 2, 128),
        in_specs=[SMEM_SPEC] + [VMEM_SPEC] * 8 + [SMEM_SPEC, VMEM_SPEC],
        out_specs=VMEM_SPEC,
        scratch_shapes=[
            pltpu.VMEM((4, WIN_L * G, 256), F32),
            pltpu.VMEM((9, 2, ROWS_E, 128), BF16),
            pltpu.VMEM((9, 2, ROWS_E, 256), BF16),
            pltpu.VMEM((9, 2, ROWS_E, 256), BF16),
            pltpu.VMEM((2, 2, ROWS_E, 256), F32),
            pltpu.VMEM((2, SLABS, 256, 128), F32),
            pltpu.VMEM((2 * COLS, V, 128), F32),
            pltpu.VMEM((2 * COLS, 128), F32),
            pltpu.VMEM((2 * COLS, 128), F32),
        ],
        compiler_params=PARAMS,
        name="volume",
    )(place, above, below, cost, lift_own, lift_halo, w1, w2, derive_w, head, target[0])
    everyone = lax.all_to_all(shares, ("rows", "disp"), 0, 0, tiled=True)
    disparity, normals, loss, head_grad = pl.pallas_call(
        finish_kernel,
        out_shape=(arr(F32, 1, 2, 256), arr(F32, 3, 1, 2, 256), arr(F32, 1, 1), arr(F32, 1, V)),
        in_specs=[SMEM_SPEC, VMEM_SPEC],
        out_specs=(VMEM_SPEC, VMEM_SPEC, SMEM_SPEC, VMEM_SPEC),
        compiler_params=PARAMS,
        name="finish",
    )(place, everyone)
    return disparity, normals, loss.reshape(()), head_grad.reshape(V)


def solution(mesh):
    rows4 = P(None, "rows", None, None)
    return jax.shard_map(
        body,
        mesh=mesh,
        in_specs=(rows4, rows4, P(), P(), P(), P(), P(None, "rows", None)),
        out_specs=(P(None, "rows", None), P(None, None, "rows", None), P(), P()),
        check_vma=False,
    )
```

```python
import math

import jax
import jax.numpy as jnp
from jax import lax
from jax.experimental import pallas as pl
from jax.experimental.pallas import tpu as pltpu
from jax.sharding import PartitionSpec as P

G = 8
V = 32
DISP = 104
SLABS = 7
PART = 16
ROWS_E = 17 * PART
ROWS = (ROWS_E, ROWS_E - PART)
COLS = 64
WIN_L = COLS + 4
WIN_R = COLS + 3 + DISP
BASE = COLS + 1
OWN, HALO = (2, 3), (0, 1, 4, 5)
K_OWN = 3 * 2 * 128
K_HALO = 3 * 2 * 256
NT = (((1,), (1,)), ((), ()))
TN = (((0,), (0,)), ((), ()))
F32 = jnp.float32
BF16 = jnp.bfloat16


def iota(shape, dim):
    return lax.broadcasted_iota(jnp.int32, shape, dim)


def dot(a, b):
    return jnp.dot(a, b, preferred_element_type=F32)


def dot_nt(a, b):
    return lax.dot_general(a, b, NT, preferred_element_type=F32)


def dot_tn(a, b):
    return lax.dot_general(a, b, TN, preferred_element_type=F32)


def one_hot(condition):
    return jnp.where(condition, 1.0, 0.0).astype(BF16)


def order_matrix():
    rows = iota((9 * PART, 128), 0)
    lanes = iota((9 * PART, 128), 1)
    wanted = (rows % PART) * SLABS + rows // PART - 1
    return one_hot((wanted == lanes) & (wanted >= 0) & (wanted < DISP))


def group_mask():
    ch = iota((WIN_L * G, 224), 1)
    grp = iota((WIN_L * G, 224), 0) % G
    return jnp.where((ch >= grp * 28) & (ch < grp * 28 + 28), 1.0, 0.0)


def correlate(left, right, pick_left, pick_right, mask):
    spread = (dot_nt(pick_left, left) * mask).astype(BF16)
    turned = dot(right, pick_right).astype(BF16)
    return dot(spread, turned) * (1.0 / 28.0)


def store_lifted(y, lifted, quad, width):
    at = pl.ds(pl.multiple_of(quad * PART, PART), PART)
    for slab in range(9):
        for parity in range(2):
            y[slab, parity, at, :] = lifted[
                slab * PART : (slab + 1) * PART, parity * width : (parity + 1) * width
            ]


def window_of(y, slab, parity):
    spans = ((0, 0, ROWS_E), (1, 0, ROWS_E)) if parity == 0 else ((1, 0, 256), (0, PART, ROWS_E))
    return jnp.concatenate(
        [y[slab - 1 + dq, at, low:high] for dq in range(3) for at, low, high in spans], axis=1
    )


def cost_of_quad(corr, quad, slots):
    pieces = []
    for wi in range(4):
        col = quad * 4 + wi
        shift = lax.rem(256 - (WIN_L - 1) + col, 256)
        for slot in range(slots):
            block = corr[slot, pl.ds(pl.multiple_of(col * G, G), G), :]
            pieces.append(pltpu.roll(block, shift, 1)[:, :128])
    return jnp.concatenate(pieces, axis=0)


def fetch(sources, targets, sems):
    copies = [
        pltpu.make_async_copy(source, target, sems.at[k])
        for k, (source, target) in enumerate(zip(sources, targets))
    ]
    for copy in copies:
        copy.start()
    return copies


def pack_kernel(place, left_hbm, right_hbm, out, left, right, sems):
    copies = fetch((left_hbm, right_hbm), (left, right), sems)
    col0 = lax.rem(place[0] + 2, 4) * COLS
    lane = iota((2 * 224, 256), 1)
    l_col, r_col = lane + col0 - 2, lane + col0 - (WIN_L + DISP + 1)
    copies[0].wait()
    l_all = left[...].reshape(2 * 224, 256).astype(F32)
    l_all = pltpu.roll(l_all, lax.rem(258 - col0, 256), 1)
    l_all = jnp.where((l_col >= 0) & (l_col < 256), l_all, 0.0)
    copies[1].wait()
    r_all = right[...].reshape(2 * 224, 256).astype(F32)
    r_all = pltpu.roll(r_all, lax.rem(256 + WIN_L + DISP + 1 - col0, 256), 1)
    r_all = jnp.where((r_col >= 0) & (r_col < 256) & (lane < WIN_L + WIN_R), r_all, 0.0)
    out[...] = jnp.where(lane < WIN_L, l_all, r_all).astype(BF16).reshape(2, 224, 256)


def block_diagonal(small, times):
    size = 32 * times
    up = one_hot(iota((size, 32), 0) % 32 == iota((size, 32), 1))
    across = one_hot(iota((32, size), 0) == iota((32, size), 1) % 32)
    tiled = dot(dot(up, small).astype(BF16), across)
    same = iota((size, size), 0) // 32 == iota((size, size), 1) // 32
    return jnp.where(same, tiled, 0.0).astype(BF16)


def place_taps(taps, group, depth, col, position, cols_out, rows_out):
    halves = []
    for half in range(2):
        total = jnp.zeros((V, 128), BF16)
        for spot in range(4):
            index = half * 4 + spot
            out_col, out_row = index // rows_out, index % rows_out
            j, k = position - out_row, col - out_col
            if 0 <= j < 3 and 0 <= k < 3:
                total = jnp.where(group == spot, taps[(depth * 3 + j) * 3 + k], total)
        halves.append(total)
    return jnp.concatenate(halves, axis=1)


def prep_kernel(
    place,
    left_hbm,
    right_hbm,
    conv_hbm,
    stem_hbm,
    attn_hbm,
    y_own,
    partial,
    w1,
    w2,
    lift_halo,
    derive_w,
    mask,
    order,
    pick_halo,
    turn_halo,
    left,
    right,
    conv,
    stem,
    attn,
    corr,
    w1_own,
    lift_own,
    sems,
):
    copies = fetch(
        (left_hbm, right_hbm, conv_hbm, stem_hbm, attn_hbm), (left, right, conv, stem, attn), sems
    )
    disp_index, row_index, row_last = place[0], place[1], place[2]
    col0 = disp_index * COLS

    order[...] = order_matrix()
    shape = (WIN_L * G, 256)
    u = iota((256, 256), 1)
    lane = iota((256, 256), 0)
    pick_halo[...] = one_hot(iota(shape, 1) == iota(shape, 0) // G)
    turn_halo[...] = one_hot((lane == WIN_L + WIN_R - 1 - u) & (u < WIN_R))

    rows = iota((ROWS_E, 256), 0)
    lanes = iota((ROWS_E, 256), 1)
    wo, ro = lanes // 128, (lanes // 32) % 4
    inside = ((ro > 0) | (row_index > 0)) & ((ro < 3) | (row_index < row_last))
    first = (rows // PART == 0) & (wo == 0) & (disp_index == 0)
    last = (rows // PART == 16) & (wo == 1) & (disp_index == 3)
    even_ok = inside & ~first & ~last
    part = rows % PART
    for tail in range(2):
        deep = part < 15 - tail
        mask[tail, 0] = jnp.where(even_ok & deep, 1.0, 0.0)
        mask[tail, 1] = jnp.where(inside & deep, 1.0, 0.0)
    for copy in copies:
        copy.wait()

    copies = one_hot(iota((V, 128), 0) == iota((V, 128), 1) % V)
    group = iota((V, 128), 1) // V
    for layer in range(2):
        taps = [dot_tn(conv[layer * 27 + tap], copies).astype(BF16) for tap in range(27)]
        for depth in range(3):
            if layer == 0:
                for a in range(2):
                    for wpar in range(2):
                        for out, width, spots in ((w1_own, 128, OWN), (w1, 256, HALO)):
                            for slot, position in enumerate(spots):
                                row = (depth * 2 + a) * width + (wpar * len(spots) + slot) * V
                                out[row : row + V, :] = place_taps(
                                    taps, group, depth, a * 2 + wpar, position, 2, 4
                                )
            else:
                for col in range(6):
                    for slot in range(4):
                        row = ((depth * 6 + col) * 4 + slot) * V
                        w2[row : row + V, :] = place_taps(taps, group, depth, col, slot, 4, 2)
    for out, slots in ((lift_own, 2), (lift_halo, 4)):
        rows, cols = 128, 4 * slots * V
        up = one_hot(iota((rows, G), 0) % G == iota((rows, G), 1))
        across = one_hot(iota((V, cols), 0) == iota((V, cols), 1) % V)
        tiled = dot(dot(up, stem[...]).astype(BF16), across)
        same = iota((rows, cols), 0) // G == iota((rows, cols), 1) // V
        out[...] = jnp.where(same, tiled, 0.0).astype(BF16)
    folded = (dot_tn(attn[1], attn[0]) * (1.0 / math.sqrt(V))).astype(BF16)
    derive_w[0:128, :] = block_diagonal(folded, 4)
    derive_w[128:256, :] = block_diagonal(attn[2], 4)

    pick_left = one_hot(iota(shape, 1) == iota(shape, 0) // G + col0 - 2)
    pick_right = one_hot((lane == col0 + BASE - u) & (u < WIN_R))
    channels = group_mask()
    for row in range(2):
        corr[row] = correlate(left[row], right[row], pick_left, pick_right, channels)

    def lift_quad(quad, carry):
        own = jnp.concatenate([cost_of_quad(corr, quad, 2), jnp.zeros((64, 128), F32)], axis=0)
        costs = dot(order[...], own.T.astype(BF16)).astype(BF16)
        store_lifted(y_own, dot(costs, lift_own[...]).astype(BF16), quad, 128)
        return carry

    lax.fori_loop(0, 17, lift_quad, 0, unroll=17)

    def conv1(slab, carry):
        for parity in range(2):
            partial[slab - 1, parity, 0 : ROWS[parity]] = dot(
                window_of(y_own, slab, parity), w1_own[...]
            )
        return carry

    lax.fori_loop(1, SLABS + 1, conv1, 0, unroll=7)


def volume_kernel(
    place,
    above,
    below,
    y_own,
    partial,
    w1,
    w2,
    lift_halo,
    derive_w,
    mask,
    order,
    pick_halo,
    turn_halo,
    head,
    target,
    out,
    corr,
    y_halo,
    hidden,
    x,
    att,
    logit,
    weight,
):
    disp_index, row_index, row_last = place[0], place[1], place[2]
    col0 = disp_index * COLS

    pick_left, pick_right = pick_halo[...], turn_halo[...]
    channels = group_mask()
    for side, rows in enumerate((above, below)):
        there = row_index > 0 if side == 0 else row_index < row_last
        swap = lax.rem(row_index, 2) == 0
        kept = channels * jnp.where(there, 1.0, 0.0)
        for row in range(2):
            both = jnp.where(swap, (below, above)[side][row], (above, below)[side][row])
            corr[side * 2 + row] = correlate(both, both, pick_left, pick_right, kept)

    def lift_quad(quad, carry):
        costs = dot(order[...], cost_of_quad(corr, quad, 4).T.astype(BF16)).astype(BF16)
        store_lifted(y_halo, dot(costs, lift_halo[...]).astype(BF16), quad, 256)
        return carry

    lax.fori_loop(0, 17, lift_quad, 0, unroll=17)

    def conv1(slab, carry):
        tail = jnp.where(slab == SLABS, 1, 0)
        for parity in range(2):
            count = ROWS[parity]
            total = dot(window_of(y_halo, slab, parity), w1[...]) + partial[slab - 1, parity, 0:count]
            total = jnp.maximum(total, 0.0) * mask[tail, parity, 0:count]
            hidden[slab, parity, 0:count] = total.astype(BF16)
        return carry

    lax.fori_loop(1, SLABS + 1, conv1, 0, unroll=7)
    for parity, count in ((0, ROWS_E), (1, 256)):
        place_in = iota((count, 256), 0) % PART
        before = hidden[SLABS, parity, 0:count].astype(F32)
        before = jnp.where(place_in == 0, 0.0, pltpu.roll(before, 1, 0))
        hidden[0, parity, 0:count] = before.astype(BF16)
        after = hidden[1, parity, 0:count].astype(F32)
        after = jnp.where(place_in == PART - 1, 0.0, pltpu.roll(after, count - 1, 0))
        hidden[SLABS + 1, parity, 0:count] = after.astype(BF16)

    def conv2(slab, carry):
        pieces = []
        for dq in range(3):
            at = slab - 1 + dq
            pieces += [hidden[at, 0, 0:256], hidden[at, 1, 0:256], hidden[at, 0, PART:ROWS_E]]
        total = dot(jnp.concatenate(pieces, axis=1), w2[...])
        x[0, slab - 1] = total[:, :128] + y_own[slab, 1, 0:256].astype(F32)
        x[1, slab - 1] = total[:, 128:] + y_own[slab, 0, PART:ROWS_E].astype(F32)
        return carry

    lax.fori_loop(1, SLABS + 1, conv2, 0, unroll=7)

    e_row = iota((SLABS * PART, 256), 0)
    e_valid = (e_row % PART) * SLABS + e_row // PART < DISP
    head_col = jnp.zeros((V, 128), F32)
    for v in range(V):
        head_col = jnp.where(iota((V, 128), 0) == v, head[v], head_col)

    def attend(quad, carry):
        at = pl.ds(pl.multiple_of(quad * PART, PART), PART)
        for half in range(2):
            tokens = jnp.concatenate([x[half, slab, at, :] for slab in range(SLABS)], axis=0)
            rounded = tokens.astype(BF16)
            turned = jnp.concatenate([tokens, jnp.zeros((PART, 128), F32)], axis=0).T
            derived = dot(derive_w[...], turned.astype(BF16)).astype(BF16)
            queries, values = derived[:128], derived[128:]
            chosen = []
            for px in range(4):
                at_px = slice(px * 32, px * 32 + 32)
                above_px = jnp.zeros((at_px.start, 128), BF16)
                below_px = jnp.zeros((128 - at_px.stop, 128), BF16)
                pieces = [above_px, queries[at_px], below_px]
                chosen.append(jnp.concatenate([k for k in pieces if k.shape[0]], axis=0))
            wide = dot(rounded, jnp.concatenate(chosen, axis=1))
            for pair in range(2):
                scores = wide[:, pair * 256 : pair * 256 + 256]
                scores = jnp.where(e_valid, scores, -1e30)
                top = jnp.max(scores, axis=0, keepdims=True)
                grown = jnp.exp(scores - top)
                scale = 1.0 / jnp.sum(grown, axis=0, keepdims=True)
                chances = (grown * scale).astype(BF16)
                chances = jnp.concatenate([chances, jnp.zeros((PART, 256), BF16)], axis=0)
                mixed = dot(values[pair * 64 : pair * 64 + 64], chances)
                for row in range(2):
                    px = pair * 2 + row
                    attended = (
                        turned[px * 32 : px * 32 + 32]
                        + mixed[row * 32 : row * 32 + 32, row * 128 : row * 128 + 128]
                    )
                    index = row * COLS + quad * 4 + half * 2 + pair
                    att[index] = attended
                    logit[pl.ds(index, 1), :] = jnp.sum(
                        attended * head_col, axis=0, keepdims=True
                    )
        return carry

    lax.fori_loop(0, 16, attend, 0, unroll=8)

    slot_lane = iota((128, 128), 1)
    depth = (slot_lane % PART) * SLABS + slot_lane // PART
    valid = (slot_lane < SLABS * PART) & (depth < DISP)
    depth_f = depth.astype(F32)
    logits = jnp.where(valid, logit[...], -1e30)
    grown = jnp.where(valid, jnp.exp(logits - jnp.max(logits, axis=1, keepdims=True)), 0.0)
    prob = grown / jnp.sum(grown, axis=1, keepdims=True)
    disparity = jnp.sum(prob * depth_f, axis=1, keepdims=True)
    disp_row = jnp.broadcast_to(disparity, (128, 128)).T[0:1]
    turned = [pltpu.roll(target[...], lax.rem(256 + row * COLS - col0, 256), 1) for row in range(2)]
    lane_row = iota((1, 128), 1)
    wanted = jnp.where(lane_row < COLS, turned[0][0:1, :128], turned[1][1:2, :128])
    residual = disp_row - wanted
    size = jnp.abs(residual)
    huber = jnp.where(size < 1.0, 0.5 * residual * residual, size - 0.5)
    pixels = 1.0 / ((row_last + 1) * (2 * 4 * COLS)).astype(F32)
    loss = jnp.sum(huber, axis=1, keepdims=True) * pixels
    slope = jnp.clip(residual, -1.0, 1.0) * pixels
    slope_col = jnp.broadcast_to(slope, (128, 128)).T
    weight[...] = slope_col * prob * (depth_f - disparity)

    def gather(block, total):
        for k in range(8):
            px = block * 8 + k
            total += att[px] * weight[pl.ds(px, 1), :]
        return total

    total = lax.fori_loop(0, 16, gather, jnp.zeros((V, 128), F32))
    padded = jnp.concatenate([total, jnp.zeros((128 - V, 128), F32)], axis=0)
    grads = jnp.sum(padded.T, axis=0, keepdims=True)
    sums = jnp.where(lane_row == V, loss, grads)
    out[...] = jnp.broadcast_to(jnp.concatenate([disp_row, sums], axis=0)[None], (128, 2, 128))


def finish_kernel(place, everyone, disparity, normals, loss, head_grad):
    row_index, row_last = place[1], place[2]
    sums = jnp.sum(everyone[...], axis=0)[1:2]
    head_grad[...] = sums[:, :V]
    loss[0, 0] = jnp.sum(jnp.where(iota((1, 128), 1) == V, sums, 0.0))
    low = iota((8, 128), 1) < COLS
    bands = []
    for band in range(2):
        start = jnp.minimum(row_index + band, row_last) * 4
        lines = [
            jnp.broadcast_to(everyone[start + k][0:1], (8, 128)) for k in range(4)
        ]
        swapped = [pltpu.roll(line, COLS, 1) for line in lines]
        tops = [jnp.where(low, lines[k], swapped[k + 1]) for k in (0, 2)]
        bottoms = [jnp.where(low, swapped[k], lines[k + 1]) for k in (0, 2)]
        bands += [jnp.concatenate(tops, axis=1), jnp.concatenate(bottoms, axis=1)]
    top, bottom, follow = bands[0], bands[1], bands[2]
    step = jnp.where(row_index < row_last, 1.0, 0.0)
    lane = iota((8, 256), 1)
    for row, (here, below, scale) in enumerate(((top, bottom, 1.0), (bottom, follow, step))):
        downward = (below - here) * scale
        across = jnp.where(lane < 255, pltpu.roll(here, 255, 1) - here, 0.0)
        inverse = 1.0 / jnp.sqrt(across * across + downward * downward + 1.0)
        disparity[0, row : row + 1, :] = here[0:1]
        normals[0, 0, row : row + 1, :] = (-across * inverse)[0:1]
        normals[1, 0, row : row + 1, :] = (-downward * inverse)[0:1]
        normals[2, 0, row : row + 1, :] = inverse[0:1]


VMEM_SPEC = pl.BlockSpec(memory_space=pltpu.VMEM)
HBM_SPEC = pl.BlockSpec(memory_space=pltpu.HBM)
SMEM_SPEC = pl.BlockSpec(memory_space=pltpu.SMEM)
PARAMS = pltpu.CompilerParams(vmem_limit_bytes=24 * 1024 * 1024)


def in_hbm(x):
    return pltpu.with_memory_space_constraint(x, pltpu.HBM)


def arr(dtype, *shape):
    return jax.ShapeDtypeStruct(shape, dtype)


def body(left, right, stem, conv, attn, head, target):
    disp_index = lax.axis_index("disp")
    row_index = lax.axis_index("rows")
    row_count = lax.axis_size("rows")
    left, right = left[0], right[0]
    place = jnp.stack([disp_index, row_index, jnp.int32(row_count - 1)]).astype(jnp.int32)
    window = pl.pallas_call(
        pack_kernel,
        out_shape=arr(BF16, 2, 224, 256),
        in_specs=[SMEM_SPEC, HBM_SPEC, HBM_SPEC],
        out_specs=VMEM_SPEC,
        scratch_shapes=[
            pltpu.VMEM((2, 224, 256), BF16),
            pltpu.VMEM((2, 224, 256), BF16),
            pltpu.SemaphoreType.DMA((2,)),
        ],
        compiler_params=PARAMS,
        name="pack",
    )(place, in_hbm(left), in_hbm(right))
    pairs = (
        [(r, r ^ 1) for r in range(row_count)],
        [(r, (((r + 1) ^ 1) - 1) % row_count) for r in range(row_count)],
    )
    above, below = [
        lax.ppermute(
            window,
            ("rows", "disp"),
            [(a * 4 + k, b * 4 + (k + 2) % 4) for a, b in pair for k in range(4)],
        )
        for pair in pairs
    ]
    made = pl.pallas_call(
        prep_kernel,
        out_shape=(
            arr(BF16, 9, 2, ROWS_E, 128),
            arr(F32, SLABS, 2, ROWS_E, 256),
            arr(BF16, K_HALO, 256),
            arr(BF16, 3 * K_OWN, 256),
            arr(BF16, 128, 512),
            arr(BF16, 256, 128),
            arr(F32, 2, 2, ROWS_E, 256),
            arr(BF16, 9 * PART, 128),
            arr(BF16, WIN_L * G, 256),
            arr(BF16, 256, 256),
        ),
        in_specs=[SMEM_SPEC] + [HBM_SPEC] * 5,
        out_specs=(VMEM_SPEC,) * 10,
        scratch_shapes=[
            pltpu.VMEM((2, 224, 256), BF16),
            pltpu.VMEM((2, 224, 256), BF16),
            pltpu.VMEM((54, V, V), BF16),
            pltpu.VMEM((G, V), BF16),
            pltpu.VMEM((3, V, V), BF16),
            pltpu.VMEM((2, WIN_L * G, 256), F32),
            pltpu.VMEM((K_OWN, 256), BF16),
            pltpu.VMEM((128, 256), BF16),
            pltpu.SemaphoreType.DMA((5,)),
        ],
        compiler_params=PARAMS,
        cost_estimate=pl.CostEstimate(flops=6 * 10**9, bytes_accessed=4 * 10**6, transcendentals=0),
        name="prep",
    )(
        place,
        in_hbm(left),
        in_hbm(right),
        in_hbm(conv.transpose(0, 2, 3, 4, 1, 5).reshape(54, V, V)),
        in_hbm(stem.T),
        in_hbm(attn),
    )
    shares = pl.pallas_call(
        volume_kernel,
        out_shape=arr(F32, 128, 2, 128),
        in_specs=[SMEM_SPEC] + [VMEM_SPEC] * 12 + [SMEM_SPEC, VMEM_SPEC],
        out_specs=VMEM_SPEC,
        scratch_shapes=[
            pltpu.VMEM((4, WIN_L * G, 256), F32),
            pltpu.VMEM((9, 2, ROWS_E, 256), BF16),
            pltpu.VMEM((9, 2, ROWS_E, 256), BF16),
            pltpu.VMEM((2, SLABS, 256, 128), F32),
            pltpu.VMEM((2 * COLS, V, 128), F32),
            pltpu.VMEM((2 * COLS, 128), F32),
            pltpu.VMEM((2 * COLS, 128), F32),
        ],
        compiler_params=PARAMS,
        name="volume",
    )(place, above, below, *made, head, target[0])
    everyone = lax.all_to_all(shares, ("rows", "disp"), 0, 0, tiled=True)
    disparity, normals, loss, head_grad = pl.pallas_call(
        finish_kernel,
        out_shape=(arr(F32, 1, 2, 256), arr(F32, 3, 1, 2, 256), arr(F32, 1, 1), arr(F32, 1, V)),
        in_specs=[SMEM_SPEC, VMEM_SPEC],
        out_specs=(VMEM_SPEC, VMEM_SPEC, SMEM_SPEC, VMEM_SPEC),
        compiler_params=PARAMS,
        name="finish",
    )(place, everyone)
    return disparity, normals, loss.reshape(()), head_grad.reshape(V)


def solution(mesh):
    rows4 = P(None, "rows", None, None)
    return jax.shard_map(
        body,
        mesh=mesh,
        in_specs=(rows4, rows4, P(), P(), P(), P(), P(None, "rows", None)),
        out_specs=(P(None, "rows", None), P(None, None, "rows", None), P(), P()),
        check_vma=False,
    )
```

```python
import math

import jax
import jax.numpy as jnp
from jax import lax
from jax.experimental import pallas as pl
from jax.experimental.pallas import tpu as pltpu
from jax.sharding import PartitionSpec as P

G = 8
V = 32
DISP = 104
SLABS = 7
PART = 16
ROWS_E = 17 * PART
ROWS = (ROWS_E, ROWS_E - PART)
COLS = 64
WIN_L = COLS + 4
WIN_R = COLS + 3 + DISP
BASE = COLS + 1
OWN, ABOVE, BELOW = (2, 3), (0, 1), (4, 5)
K_OWN = 3 * 2 * 128
NT = (((1,), (1,)), ((), ()))
TN = (((0,), (0,)), ((), ()))
F32 = jnp.float32
BF16 = jnp.bfloat16


def iota(shape, dim):
    return lax.broadcasted_iota(jnp.int32, shape, dim)


def dot(a, b):
    return jnp.dot(a, b, preferred_element_type=F32)


def dot_nt(a, b):
    return lax.dot_general(a, b, NT, preferred_element_type=F32)


def dot_tn(a, b):
    return lax.dot_general(a, b, TN, preferred_element_type=F32)


def one_hot(condition):
    return jnp.where(condition, 1.0, 0.0).astype(BF16)


def order_matrix():
    rows = iota((9 * PART, 128), 0)
    lanes = iota((9 * PART, 128), 1)
    wanted = (rows % PART) * SLABS + rows // PART - 1
    return one_hot((wanted == lanes) & (wanted >= 0) & (wanted < DISP))


def group_mask():
    ch = iota((WIN_L * G, 224), 1)
    grp = iota((WIN_L * G, 224), 0) % G
    return jnp.where((ch >= grp * 28) & (ch < grp * 28 + 28), 1.0, 0.0)


def correlate(left, right, pick_left, pick_right, mask):
    spread = (dot_nt(pick_left, left) * mask).astype(BF16)
    turned = dot(right, pick_right).astype(BF16)
    return dot(spread, turned) * (1.0 / 28.0)


def store_lifted(y, lifted, quad, width):
    at = pl.ds(pl.multiple_of(quad * PART, PART), PART)
    for slab in range(9):
        for parity in range(2):
            y[slab, parity, at, :] = lifted[
                slab * PART : (slab + 1) * PART, parity * width : (parity + 1) * width
            ]


def window_of(y, slab, parity):
    spans = ((0, 0, ROWS_E), (1, 0, ROWS_E)) if parity == 0 else ((1, 0, 256), (0, PART, ROWS_E))
    return jnp.concatenate(
        [y[slab - 1 + dq, at, low:high] for dq in range(3) for at, low, high in spans], axis=1
    )


def cost_of_quad(corr, quad, slots):
    pieces = []
    for wi in range(4):
        col = quad * 4 + wi
        shift = lax.rem(256 - (WIN_L - 1) + col, 256)
        for slot in range(slots):
            block = corr[slot, pl.ds(pl.multiple_of(col * G, G), G), :]
            pieces.append(pltpu.roll(block, shift, 1)[:, :128])
    return jnp.concatenate(pieces, axis=0)


def fetch(sources, targets, sems):
    copies = [
        pltpu.make_async_copy(source, target, sems.at[k])
        for k, (source, target) in enumerate(zip(sources, targets))
    ]
    for copy in copies:
        copy.start()
    return copies


def lift_rows(corr, y, order, lift_w):
    def lift_quad(quad, carry):
        cost = jnp.concatenate([cost_of_quad(corr, quad, 2), jnp.zeros((64, 128), F32)], axis=0)
        costs = dot(order[...], cost.T.astype(BF16)).astype(BF16)
        store_lifted(y, dot(costs, lift_w[...]).astype(BF16), quad, 128)
        return carry

    lax.fori_loop(0, 17, lift_quad, 0, unroll=17)


def pack_kernel(place, left_hbm, right_hbm, out, left, right, sems):
    copies = fetch((left_hbm, right_hbm), (left, right), sems)
    col0 = lax.rem(place[0] + 2, 4) * COLS
    lane = iota((2 * 224, 256), 1)
    l_col, r_col = lane + col0 - 2, lane + col0 - (WIN_L + DISP + 1)
    copies[0].wait()
    l_all = left[...].reshape(2 * 224, 256).astype(F32)
    l_all = pltpu.roll(l_all, lax.rem(258 - col0, 256), 1)
    l_all = jnp.where((l_col >= 0) & (l_col < 256), l_all, 0.0)
    copies[1].wait()
    r_all = right[...].reshape(2 * 224, 256).astype(F32)
    r_all = pltpu.roll(r_all, lax.rem(256 + WIN_L + DISP + 1 - col0, 256), 1)
    r_all = jnp.where((r_col >= 0) & (r_col < 256) & (lane < WIN_L + WIN_R), r_all, 0.0)
    out[...] = jnp.where(lane < WIN_L, l_all, r_all).astype(BF16).reshape(2, 224, 256)


def block_diagonal(small, times):
    size = 32 * times
    up = one_hot(iota((size, 32), 0) % 32 == iota((size, 32), 1))
    across = one_hot(iota((32, size), 0) == iota((32, size), 1) % 32)
    tiled = dot(dot(up, small).astype(BF16), across)
    same = iota((size, size), 0) // 32 == iota((size, size), 1) // 32
    return jnp.where(same, tiled, 0.0).astype(BF16)


def place_taps(taps, group, depth, col, position, cols_out, rows_out):
    halves = []
    for half in range(2):
        total = jnp.zeros((V, 128), BF16)
        for spot in range(4):
            index = half * 4 + spot
            out_col, out_row = index // rows_out, index % rows_out
            j, k = position - out_row, col - out_col
            if 0 <= j < 3 and 0 <= k < 3:
                total = jnp.where(group == spot, taps[(depth * 3 + j) * 3 + k], total)
        halves.append(total)
    return jnp.concatenate(halves, axis=1)


def prep_kernel(
    place,
    left_hbm,
    right_hbm,
    conv_hbm,
    stem_hbm,
    attn_hbm,
    y_own,
    partial,
    w1,
    w2,
    lift_w,
    derive_w,
    mask,
    order,
    pick_halo,
    turn_halo,
    left,
    right,
    conv,
    stem,
    attn,
    corr,
    w1_own,
    sems,
):
    copies = fetch(
        (left_hbm, right_hbm, conv_hbm, stem_hbm, attn_hbm), (left, right, conv, stem, attn), sems
    )
    disp_index, row_index, row_last = place[0], place[1], place[2]
    col0 = disp_index * COLS

    order[...] = order_matrix()
    shape = (WIN_L * G, 256)
    u = iota((256, 256), 1)
    lane = iota((256, 256), 0)
    pick_halo[...] = one_hot(iota(shape, 1) == iota(shape, 0) // G)
    turn_halo[...] = one_hot((lane == WIN_L + WIN_R - 1 - u) & (u < WIN_R))

    rows = iota((ROWS_E, 256), 0)
    lanes = iota((ROWS_E, 256), 1)
    wo, ro = lanes // 128, (lanes // 32) % 4
    inside = ((ro > 0) | (row_index > 0)) & ((ro < 3) | (row_index < row_last))
    first = (rows // PART == 0) & (wo == 0) & (disp_index == 0)
    last = (rows // PART == 16) & (wo == 1) & (disp_index == 3)
    even_ok = inside & ~first & ~last
    part = rows % PART
    for tail in range(2):
        deep = part < 15 - tail
        mask[tail, 0] = jnp.where(even_ok & deep, 1.0, 0.0)
        mask[tail, 1] = jnp.where(inside & deep, 1.0, 0.0)
    for copy in copies:
        copy.wait()

    above_at = jnp.where(lax.rem(row_index, 2) == 0, K_OWN, 0)
    copies = one_hot(iota((V, 128), 0) == iota((V, 128), 1) % V)
    group = iota((V, 128), 1) // V
    for layer in range(2):
        taps = [dot_tn(conv[layer * 27 + tap], copies).astype(BF16) for tap in range(27)]
        for depth in range(3):
            if layer == 0:
                for a in range(2):
                    for wpar in range(2):
                        at = (depth * 2 + a) * 128 + wpar * 64
                        for slot in range(2):
                            for out, base, spots in (
                                (w1_own, 0, OWN),
                                (w1, above_at, ABOVE),
                                (w1, K_OWN - above_at, BELOW),
                            ):
                                row = pl.multiple_of(base + at + slot * V, V)
                                out[pl.ds(row, V), :] = place_taps(
                                    taps, group, depth, a * 2 + wpar, spots[slot], 2, 4
                                )
            else:
                for col in range(6):
                    for slot in range(4):
                        row = ((depth * 6 + col) * 4 + slot) * V
                        w2[row : row + V, :] = place_taps(taps, group, depth, col, slot, 4, 2)
    for out in (lift_w,):
        rows, cols = 128, 256
        up = one_hot(iota((rows, G), 0) % G == iota((rows, G), 1))
        across = one_hot(iota((V, cols), 0) == iota((V, cols), 1) % V)
        tiled = dot(dot(up, stem[...]).astype(BF16), across)
        same = iota((rows, cols), 0) // G == iota((rows, cols), 1) // V
        out[...] = jnp.where(same, tiled, 0.0).astype(BF16)
    folded = (dot_tn(attn[1], attn[0]) * (1.0 / math.sqrt(V))).astype(BF16)
    derive_w[0:128, :] = block_diagonal(folded, 4)
    derive_w[128:256, :] = block_diagonal(attn[2], 4)

    pick_left = one_hot(iota(shape, 1) == iota(shape, 0) // G + col0 - 2)
    pick_right = one_hot((lane == col0 + BASE - u) & (u < WIN_R))
    channels = group_mask()
    for row in range(2):
        corr[row] = correlate(left[row], right[row], pick_left, pick_right, channels)

    lift_rows(corr, y_own, order, lift_w)

    def conv1(slab, carry):
        for parity in range(2):
            partial[slab - 1, parity, 0 : ROWS[parity]] = dot(
                window_of(y_own, slab, parity), w1_own[...]
            )
        return carry

    lax.fori_loop(1, SLABS + 1, conv1, 0, unroll=7)


def first_kernel(place, rows, before, w1, lift_w, order, pick_halo, turn_halo, partial, corr, y):
    channels = group_mask()
    for row in range(2):
        corr[row] = correlate(rows[row], rows[row], pick_halo[...], turn_halo[...], channels)
    lift_rows(corr, y, order, lift_w)

    def conv1(slab, carry):
        for parity in range(2):
            count = ROWS[parity]
            partial[slab - 1, parity, 0:count] = (
                dot(window_of(y, slab, parity), w1[0:K_OWN]) + before[slab - 1, parity, 0:count]
            )
        return carry

    lax.fori_loop(1, SLABS + 1, conv1, 0, unroll=7)


def volume_kernel(
    place,
    rows,
    y_own,
    partial,
    w1,
    w2,
    lift_w,
    derive_w,
    mask,
    order,
    pick_halo,
    turn_halo,
    head,
    target,
    out,
    corr,
    y_second,
    hidden,
    x,
    att,
    logit,
    weight,
):
    disp_index, row_index, row_last = place[0], place[1], place[2]
    col0 = disp_index * COLS

    there = (row_index > 0) & (row_index < row_last)
    kept = group_mask() * jnp.where(there, 1.0, 0.0)
    for row in range(2):
        corr[row] = correlate(rows[row], rows[row], pick_halo[...], turn_halo[...], kept)
    lift_rows(corr, y_second, order, lift_w)

    def conv1(slab, carry):
        tail = jnp.where(slab == SLABS, 1, 0)
        for parity in range(2):
            count = ROWS[parity]
            total = dot(window_of(y_second, slab, parity), w1[K_OWN:]) + partial[slab - 1, parity, 0:count]
            total = jnp.maximum(total, 0.0) * mask[tail, parity, 0:count]
            hidden[slab, parity, 0:count] = total.astype(BF16)
        return carry

    lax.fori_loop(1, SLABS + 1, conv1, 0, unroll=7)
    for parity, count in ((0, ROWS_E), (1, 256)):
        place_in = iota((count, 256), 0) % PART
        before = hidden[SLABS, parity, 0:count].astype(F32)
        before = jnp.where(place_in == 0, 0.0, pltpu.roll(before, 1, 0))
        hidden[0, parity, 0:count] = before.astype(BF16)
        after = hidden[1, parity, 0:count].astype(F32)
        after = jnp.where(place_in == PART - 1, 0.0, pltpu.roll(after, count - 1, 0))
        hidden[SLABS + 1, parity, 0:count] = after.astype(BF16)

    def conv2(slab, carry):
        pieces = []
        for dq in range(3):
            at = slab - 1 + dq
            pieces += [hidden[at, 0, 0:256], hidden[at, 1, 0:256], hidden[at, 0, PART:ROWS_E]]
        total = dot(jnp.concatenate(pieces, axis=1), w2[...])
        x[0, slab - 1] = total[:, :128] + y_own[slab, 1, 0:256].astype(F32)
        x[1, slab - 1] = total[:, 128:] + y_own[slab, 0, PART:ROWS_E].astype(F32)
        return carry

    lax.fori_loop(1, SLABS + 1, conv2, 0, unroll=7)

    e_row = iota((SLABS * PART, 256), 0)
    e_valid = (e_row % PART) * SLABS + e_row // PART < DISP
    head_col = jnp.zeros((V, 128), F32)
    for v in range(V):
        head_col = jnp.where(iota((V, 128), 0) == v, head[v], head_col)

    def attend(quad, carry):
        at = pl.ds(pl.multiple_of(quad * PART, PART), PART)
        for half in range(2):
            tokens = jnp.concatenate([x[half, slab, at, :] for slab in range(SLABS)], axis=0)
            rounded = tokens.astype(BF16)
            turned = jnp.concatenate([tokens, jnp.zeros((PART, 128), F32)], axis=0).T
            derived = dot(derive_w[...], turned.astype(BF16)).astype(BF16)
            queries, values = derived[:128], derived[128:]
            chosen = []
            for px in range(4):
                at_px = slice(px * 32, px * 32 + 32)
                above_px = jnp.zeros((at_px.start, 128), BF16)
                below_px = jnp.zeros((128 - at_px.stop, 128), BF16)
                pieces = [above_px, queries[at_px], below_px]
                chosen.append(jnp.concatenate([k for k in pieces if k.shape[0]], axis=0))
            wide = dot(rounded, jnp.concatenate(chosen, axis=1))
            for pair in range(2):
                scores = wide[:, pair * 256 : pair * 256 + 256]
                scores = jnp.where(e_valid, scores, -1e30)
                top = jnp.max(scores, axis=0, keepdims=True)
                grown = jnp.exp(scores - top)
                scale = 1.0 / jnp.sum(grown, axis=0, keepdims=True)
                chances = (grown * scale).astype(BF16)
                chances = jnp.concatenate([chances, jnp.zeros((PART, 256), BF16)], axis=0)
                mixed = dot(values[pair * 64 : pair * 64 + 64], chances)
                for row in range(2):
                    px = pair * 2 + row
                    attended = (
                        turned[px * 32 : px * 32 + 32]
                        + mixed[row * 32 : row * 32 + 32, row * 128 : row * 128 + 128]
                    )
                    index = row * COLS + quad * 4 + half * 2 + pair
                    att[index] = attended
                    logit[pl.ds(index, 1), :] = jnp.sum(
                        attended * head_col, axis=0, keepdims=True
                    )
        return carry

    lax.fori_loop(0, 16, attend, 0, unroll=8)

    slot_lane = iota((128, 128), 1)
    depth = (slot_lane % PART) * SLABS + slot_lane // PART
    valid = (slot_lane < SLABS * PART) & (depth < DISP)
    depth_f = depth.astype(F32)
    logits = jnp.where(valid, logit[...], -1e30)
    grown = jnp.where(valid, jnp.exp(logits - jnp.max(logits, axis=1, keepdims=True)), 0.0)
    prob = grown / jnp.sum(grown, axis=1, keepdims=True)
    disparity = jnp.sum(prob * depth_f, axis=1, keepdims=True)
    disp_row = jnp.broadcast_to(disparity, (128, 128)).T[0:1]
    turned = [pltpu.roll(target[...], lax.rem(256 + row * COLS - col0, 256), 1) for row in range(2)]
    lane_row = iota((1, 128), 1)
    wanted = jnp.where(lane_row < COLS, turned[0][0:1, :128], turned[1][1:2, :128])
    residual = disp_row - wanted
    size = jnp.abs(residual)
    huber = jnp.where(size < 1.0, 0.5 * residual * residual, size - 0.5)
    pixels = 1.0 / ((row_last + 1) * (2 * 4 * COLS)).astype(F32)
    loss = jnp.sum(huber, axis=1, keepdims=True) * pixels
    slope = jnp.clip(residual, -1.0, 1.0) * pixels
    slope_col = jnp.broadcast_to(slope, (128, 128)).T
    weight[...] = slope_col * prob * (depth_f - disparity)

    def gather(block, total):
        for k in range(8):
            px = block * 8 + k
            total += att[px] * weight[pl.ds(px, 1), :]
        return total

    total = lax.fori_loop(0, 16, gather, jnp.zeros((V, 128), F32))
    padded = jnp.concatenate([total, jnp.zeros((128 - V, 128), F32)], axis=0)
    grads = jnp.sum(padded.T, axis=0, keepdims=True)
    sums = jnp.where(lane_row == V, loss, grads)
    out[...] = jnp.broadcast_to(jnp.concatenate([disp_row, sums], axis=0)[None], (128, 2, 128))


def finish_kernel(place, everyone, disparity, normals, loss, head_grad):
    row_index, row_last = place[1], place[2]
    sums = jnp.sum(everyone[...], axis=0)[1:2]
    head_grad[...] = sums[:, :V]
    loss[0, 0] = jnp.sum(jnp.where(iota((1, 128), 1) == V, sums, 0.0))
    low = iota((8, 128), 1) < COLS
    bands = []
    for band in range(2):
        start = jnp.minimum(row_index + band, row_last) * 4
        lines = [
            jnp.broadcast_to(everyone[start + k][0:1], (8, 128)) for k in range(4)
        ]
        swapped = [pltpu.roll(line, COLS, 1) for line in lines]
        tops = [jnp.where(low, lines[k], swapped[k + 1]) for k in (0, 2)]
        bottoms = [jnp.where(low, swapped[k], lines[k + 1]) for k in (0, 2)]
        bands += [jnp.concatenate(tops, axis=1), jnp.concatenate(bottoms, axis=1)]
    top, bottom, follow = bands[0], bands[1], bands[2]
    step = jnp.where(row_index < row_last, 1.0, 0.0)
    lane = iota((8, 256), 1)
    for row, (here, below, scale) in enumerate(((top, bottom, 1.0), (bottom, follow, step))):
        downward = (below - here) * scale
        across = jnp.where(lane < 255, pltpu.roll(here, 255, 1) - here, 0.0)
        inverse = 1.0 / jnp.sqrt(across * across + downward * downward + 1.0)
        disparity[0, row : row + 1, :] = here[0:1]
        normals[0, 0, row : row + 1, :] = (-across * inverse)[0:1]
        normals[1, 0, row : row + 1, :] = (-downward * inverse)[0:1]
        normals[2, 0, row : row + 1, :] = inverse[0:1]


VMEM_SPEC = pl.BlockSpec(memory_space=pltpu.VMEM)
HBM_SPEC = pl.BlockSpec(memory_space=pltpu.HBM)
SMEM_SPEC = pl.BlockSpec(memory_space=pltpu.SMEM)
PARAMS = pltpu.CompilerParams(vmem_limit_bytes=24 * 1024 * 1024)


def in_hbm(x):
    return pltpu.with_memory_space_constraint(x, pltpu.HBM)


def arr(dtype, *shape):
    return jax.ShapeDtypeStruct(shape, dtype)


def body(left, right, stem, conv, attn, head, target):
    disp_index = lax.axis_index("disp")
    row_index = lax.axis_index("rows")
    row_count = lax.axis_size("rows")
    left, right = left[0], right[0]
    place = jnp.stack([disp_index, row_index, jnp.int32(row_count - 1)]).astype(jnp.int32)
    window = pl.pallas_call(
        pack_kernel,
        out_shape=arr(BF16, 2, 224, 256),
        in_specs=[SMEM_SPEC, HBM_SPEC, HBM_SPEC],
        out_specs=VMEM_SPEC,
        scratch_shapes=[
            pltpu.VMEM((2, 224, 256), BF16),
            pltpu.VMEM((2, 224, 256), BF16),
            pltpu.SemaphoreType.DMA((2,)),
        ],
        compiler_params=PARAMS,
        name="pack",
    )(place, in_hbm(left), in_hbm(right))
    pairs = (
        [(r, r ^ 1) for r in range(row_count)],
        [(r, (((r + 1) ^ 1) - 1) % row_count) for r in range(row_count)],
    )
    first, second = [
        lax.ppermute(
            window,
            ("rows", "disp"),
            [(a * 4 + k, b * 4 + (k + 2) % 4) for a, b in pair for k in range(4)],
        )
        for pair in pairs
    ]
    y_own, partial, w1, w2, lift_w, derive_w, mask, order, pick_halo, turn_halo = pl.pallas_call(
        prep_kernel,
        out_shape=(
            arr(BF16, 9, 2, ROWS_E, 128),
            arr(F32, SLABS, 2, ROWS_E, 256),
            arr(BF16, 2 * K_OWN, 256),
            arr(BF16, 3 * K_OWN, 256),
            arr(BF16, 128, 256),
            arr(BF16, 256, 128),
            arr(F32, 2, 2, ROWS_E, 256),
            arr(BF16, 9 * PART, 128),
            arr(BF16, WIN_L * G, 256),
            arr(BF16, 256, 256),
        ),
        in_specs=[SMEM_SPEC] + [HBM_SPEC] * 5,
        out_specs=(VMEM_SPEC,) * 10,
        scratch_shapes=[
            pltpu.VMEM((2, 224, 256), BF16),
            pltpu.VMEM((2, 224, 256), BF16),
            pltpu.VMEM((54, V, V), BF16),
            pltpu.VMEM((G, V), BF16),
            pltpu.VMEM((3, V, V), BF16),
            pltpu.VMEM((2, WIN_L * G, 256), F32),
            pltpu.VMEM((K_OWN, 256), BF16),
            pltpu.SemaphoreType.DMA((5,)),
        ],
        compiler_params=PARAMS,
        cost_estimate=pl.CostEstimate(flops=6 * 10**9, bytes_accessed=4 * 10**6, transcendentals=0),
        name="prep",
    )(
        place,
        in_hbm(left),
        in_hbm(right),
        in_hbm(conv.transpose(0, 2, 3, 4, 1, 5).reshape(54, V, V)),
        in_hbm(stem.T),
        in_hbm(attn),
    )
    partial = pl.pallas_call(
        first_kernel,
        out_shape=arr(F32, SLABS, 2, ROWS_E, 256),
        in_specs=[SMEM_SPEC] + [VMEM_SPEC] * 7,
        out_specs=VMEM_SPEC,
        scratch_shapes=[
            pltpu.VMEM((2, WIN_L * G, 256), F32),
            pltpu.VMEM((9, 2, ROWS_E, 128), BF16),
        ],
        compiler_params=PARAMS,
        cost_estimate=pl.CostEstimate(flops=4 * 10**9, bytes_accessed=4 * 10**6, transcendentals=0),
        name="first",
    )(place, first, partial, w1, lift_w, order, pick_halo, turn_halo)
    shares = pl.pallas_call(
        volume_kernel,
        out_shape=arr(F32, 128, 2, 128),
        in_specs=[SMEM_SPEC] + [VMEM_SPEC] * 11 + [SMEM_SPEC, VMEM_SPEC],
        out_specs=VMEM_SPEC,
        scratch_shapes=[
            pltpu.VMEM((2, WIN_L * G, 256), F32),
            pltpu.VMEM((9, 2, ROWS_E, 128), BF16),
            pltpu.VMEM((9, 2, ROWS_E, 256), BF16),
            pltpu.VMEM((2, SLABS, 256, 128), F32),
            pltpu.VMEM((2 * COLS, V, 128), F32),
            pltpu.VMEM((2 * COLS, 128), F32),
            pltpu.VMEM((2 * COLS, 128), F32),
        ],
        compiler_params=PARAMS,
        name="volume",
    )(
        place,
        second,
        y_own,
        partial,
        w1,
        w2,
        lift_w,
        derive_w,
        mask,
        order,
        pick_halo,
        turn_halo,
        head,
        target[0],
    )
    everyone = lax.all_to_all(shares, ("rows", "disp"), 0, 0, tiled=True)
    disparity, normals, loss, head_grad = pl.pallas_call(
        finish_kernel,
        out_shape=(arr(F32, 1, 2, 256), arr(F32, 3, 1, 2, 256), arr(F32, 1, 1), arr(F32, 1, V)),
        in_specs=[SMEM_SPEC, VMEM_SPEC],
        out_specs=(VMEM_SPEC, VMEM_SPEC, SMEM_SPEC, VMEM_SPEC),
        compiler_params=PARAMS,
        name="finish",
    )(place, everyone)
    return disparity, normals, loss.reshape(()), head_grad.reshape(V)


def solution(mesh):
    rows4 = P(None, "rows", None, None)
    return jax.shard_map(
        body,
        mesh=mesh,
        in_specs=(rows4, rows4, P(), P(), P(), P(), P(None, "rows", None)),
        out_specs=(P(None, "rows", None), P(None, None, "rows", None), P(), P()),
        check_vma=False,
    )
```

```python
import math

import jax
import jax.numpy as jnp
from jax import lax
from jax.experimental import pallas as pl
from jax.experimental.pallas import tpu as pltpu
from jax.sharding import PartitionSpec as P

G = 8
V = 32
DISP = 104
SLABS = 7
PART = 16
ROWS_E = 17 * PART
ROWS = (ROWS_E, ROWS_E - PART)
COLS = 64
WIN_L = COLS + 4
WIN_R = COLS + 3 + DISP
BASE = COLS + 1
OWN, ABOVE, BELOW = (2, 3), (0, 1), (4, 5)
K_OWN = 3 * 2 * 128
NT = (((1,), (1,)), ((), ()))
TN = (((0,), (0,)), ((), ()))
F32 = jnp.float32
BF16 = jnp.bfloat16


def iota(shape, dim):
    return lax.broadcasted_iota(jnp.int32, shape, dim)


def dot(a, b):
    return jnp.dot(a, b, preferred_element_type=F32)


def dot_nt(a, b):
    return lax.dot_general(a, b, NT, preferred_element_type=F32)


def dot_tn(a, b):
    return lax.dot_general(a, b, TN, preferred_element_type=F32)


def one_hot(condition):
    return jnp.where(condition, 1.0, 0.0).astype(BF16)


def order_matrix():
    rows = iota((9 * PART, 128), 0)
    lanes = iota((9 * PART, 128), 1)
    wanted = (rows % PART) * SLABS + rows // PART - 1
    return one_hot((wanted == lanes) & (wanted >= 0) & (wanted < DISP))


def group_mask():
    ch = iota((WIN_L * G, 224), 1)
    grp = iota((WIN_L * G, 224), 0) % G
    return jnp.where((ch >= grp * 28) & (ch < grp * 28 + 28), 1.0, 0.0)


def correlate(left, right, pick_left, pick_right, mask):
    spread = (dot_nt(pick_left, left) * mask).astype(BF16)
    turned = dot(right, pick_right).astype(BF16)
    return dot(spread, turned) * (1.0 / 28.0)


def store_lifted(y, lifted, quad, width):
    at = pl.ds(pl.multiple_of(quad * PART, PART), PART)
    for slab in range(9):
        for parity in range(2):
            y[slab, parity, at, :] = lifted[
                slab * PART : (slab + 1) * PART, parity * width : (parity + 1) * width
            ]


def window_of(y, slab, parity):
    spans = ((0, 0, ROWS_E), (1, 0, ROWS_E)) if parity == 0 else ((1, 0, 256), (0, PART, ROWS_E))
    return jnp.concatenate(
        [y[slab - 1 + dq, at, low:high] for dq in range(3) for at, low, high in spans], axis=1
    )


def cost_of_quad(corr, quad, slots):
    pieces = []
    for wi in range(4):
        col = quad * 4 + wi
        shift = lax.rem(256 - (WIN_L - 1) + col, 256)
        for slot in range(slots):
            block = corr[slot, pl.ds(pl.multiple_of(col * G, G), G), :]
            pieces.append(pltpu.roll(block, shift, 1)[:, :128])
    return jnp.concatenate(pieces, axis=0)


def fetch(sources, targets, sems):
    copies = [
        pltpu.make_async_copy(source, target, sems.at[k])
        for k, (source, target) in enumerate(zip(sources, targets))
    ]
    for copy in copies:
        copy.start()
    return copies


def lift_rows(corr, y, order, lift_w):
    def lift_quad(quad, carry):
        cost = jnp.concatenate([cost_of_quad(corr, quad, 2), jnp.zeros((64, 128), F32)], axis=0)
        costs = dot(order[...], cost.T.astype(BF16)).astype(BF16)
        store_lifted(y, dot(costs, lift_w[...]).astype(BF16), quad, 128)
        return carry

    lax.fori_loop(0, 17, lift_quad, 0, unroll=17)


def pack_kernel(place, left_hbm, right_hbm, out, left, right, sems):
    copies = fetch((left_hbm, right_hbm), (left, right), sems)
    col0 = lax.rem(place[0] + 2, 4) * COLS
    lane = iota((2 * 224, 256), 1)
    l_col, r_col = lane + col0 - 2, lane + col0 - (WIN_L + DISP + 1)
    copies[0].wait()
    l_all = left[...].reshape(2 * 224, 256).astype(F32)
    l_all = pltpu.roll(l_all, lax.rem(258 - col0, 256), 1)
    l_all = jnp.where((l_col >= 0) & (l_col < 256), l_all, 0.0)
    copies[1].wait()
    r_all = right[...].reshape(2 * 224, 256).astype(F32)
    r_all = pltpu.roll(r_all, lax.rem(256 + WIN_L + DISP + 1 - col0, 256), 1)
    r_all = jnp.where((r_col >= 0) & (r_col < 256) & (lane < WIN_L + WIN_R), r_all, 0.0)
    out[...] = jnp.where(lane < WIN_L, l_all, r_all).astype(BF16).reshape(2, 224, 256)


def block_diagonal(small, times):
    size = 32 * times
    up = one_hot(iota((size, 32), 0) % 32 == iota((size, 32), 1))
    across = one_hot(iota((32, size), 0) == iota((32, size), 1) % 32)
    tiled = dot(dot(up, small).astype(BF16), across)
    same = iota((size, size), 0) // 32 == iota((size, size), 1) // 32
    return jnp.where(same, tiled, 0.0).astype(BF16)


def place_taps(taps, group, depth, col, position, cols_out, rows_out):
    halves = []
    for half in range(2):
        total = jnp.zeros((V, 128), BF16)
        for spot in range(4):
            index = half * 4 + spot
            out_col, out_row = index // rows_out, index % rows_out
            j, k = position - out_row, col - out_col
            if 0 <= j < 3 and 0 <= k < 3:
                total = jnp.where(group == spot, taps[(depth * 3 + j) * 3 + k], total)
        halves.append(total)
    return jnp.concatenate(halves, axis=1)


def prep_kernel(
    place,
    left_hbm,
    right_hbm,
    conv_hbm,
    stem_hbm,
    attn_hbm,
    y_own,
    partial,
    w1,
    w2,
    lift_w,
    derive_w,
    mask,
    order,
    pick_halo,
    turn_halo,
    left,
    right,
    conv,
    stem,
    attn,
    corr,
    w1_own,
    sems,
):
    copies = fetch(
        (left_hbm, right_hbm, conv_hbm, stem_hbm, attn_hbm), (left, right, conv, stem, attn), sems
    )
    disp_index, row_index, row_last = place[0], place[1], place[2]
    col0 = disp_index * COLS

    order[...] = order_matrix()
    shape = (WIN_L * G, 256)
    u = iota((256, 256), 1)
    lane = iota((256, 256), 0)
    pick_halo[...] = one_hot(iota(shape, 1) == iota(shape, 0) // G)
    turn_halo[...] = one_hot((lane == WIN_L + WIN_R - 1 - u) & (u < WIN_R))

    rows = iota((ROWS_E, 256), 0)
    lanes = iota((ROWS_E, 256), 1)
    wo, ro = lanes // 128, (lanes // 32) % 4
    inside = ((ro > 0) | (row_index > 0)) & ((ro < 3) | (row_index < row_last))
    first = (rows // PART == 0) & (wo == 0) & (disp_index == 0)
    last = (rows // PART == 16) & (wo == 1) & (disp_index == 3)
    even_ok = inside & ~first & ~last
    part = rows % PART
    for tail in range(2):
        deep = part < 15 - tail
        mask[tail, 0] = jnp.where(even_ok & deep, 1.0, 0.0)
        mask[tail, 1] = jnp.where(inside & deep, 1.0, 0.0)
    for copy in copies:
        copy.wait()

    above_at = jnp.where(lax.rem(row_index, 2) == 0, 0, K_OWN)
    copies = one_hot(iota((V, 128), 0) == iota((V, 128), 1) % V)
    group = iota((V, 128), 1) // V
    for layer in range(2):
        taps = [dot_tn(conv[layer * 27 + tap], copies).astype(BF16) for tap in range(27)]
        for depth in range(3):
            if layer == 0:
                for a in range(2):
                    for wpar in range(2):
                        at = (depth * 2 + a) * 128 + wpar * 64
                        for slot in range(2):
                            for out, base, spots in (
                                (w1_own, 0, OWN),
                                (w1, above_at, ABOVE),
                                (w1, K_OWN - above_at, BELOW),
                            ):
                                row = pl.multiple_of(base + at + slot * V, V)
                                out[pl.ds(row, V), :] = place_taps(
                                    taps, group, depth, a * 2 + wpar, spots[slot], 2, 4
                                )
            else:
                for col in range(6):
                    for slot in range(4):
                        row = ((depth * 6 + col) * 4 + slot) * V
                        w2[row : row + V, :] = place_taps(taps, group, depth, col, slot, 4, 2)
    for out in (lift_w,):
        rows, cols = 128, 256
        up = one_hot(iota((rows, G), 0) % G == iota((rows, G), 1))
        across = one_hot(iota((V, cols), 0) == iota((V, cols), 1) % V)
        tiled = dot(dot(up, stem[...]).astype(BF16), across)
        same = iota((rows, cols), 0) // G == iota((rows, cols), 1) // V
        out[...] = jnp.where(same, tiled, 0.0).astype(BF16)
    folded = (dot_tn(attn[1], attn[0]) * (1.0 / math.sqrt(V))).astype(BF16)
    derive_w[0:128, :] = block_diagonal(folded, 4)
    derive_w[128:256, :] = block_diagonal(attn[2], 4)

    pick_left = one_hot(iota(shape, 1) == iota(shape, 0) // G + col0 - 2)
    pick_right = one_hot((lane == col0 + BASE - u) & (u < WIN_R))
    channels = group_mask()
    for row in range(2):
        corr[row] = correlate(left[row], right[row], pick_left, pick_right, channels)

    lift_rows(corr, y_own, order, lift_w)

    def conv1(slab, carry):
        for parity in range(2):
            partial[slab - 1, parity, 0 : ROWS[parity]] = dot(
                window_of(y_own, slab, parity), w1_own[...]
            )
        return carry

    lax.fori_loop(1, SLABS + 1, conv1, 0, unroll=7)


def first_kernel(place, rows, before, w1, lift_w, order, pick_halo, turn_halo, partial, corr, y):
    there = (place[1] > 0) & (place[1] < place[2])
    kept = group_mask() * jnp.where(there, 1.0, 0.0)
    for row in range(2):
        corr[row] = correlate(rows[row], rows[row], pick_halo[...], turn_halo[...], kept)
    lift_rows(corr, y, order, lift_w)

    def conv1(slab, carry):
        for parity in range(2):
            count = ROWS[parity]
            partial[slab - 1, parity, 0:count] = (
                dot(window_of(y, slab, parity), w1[0:K_OWN]) + before[slab - 1, parity, 0:count]
            )
        return carry

    lax.fori_loop(1, SLABS + 1, conv1, 0, unroll=7)


def volume_kernel(
    place,
    rows,
    y_own,
    partial,
    w1,
    w2,
    lift_w,
    derive_w,
    mask,
    order,
    pick_halo,
    turn_halo,
    head,
    target,
    out,
    corr,
    y_second,
    hidden,
    x,
    att,
    logit,
    weight,
):
    disp_index, row_index, row_last = place[0], place[1], place[2]
    col0 = disp_index * COLS

    channels = group_mask()
    for row in range(2):
        corr[row] = correlate(rows[row], rows[row], pick_halo[...], turn_halo[...], channels)
    lift_rows(corr, y_second, order, lift_w)

    def conv1(slab, carry):
        tail = jnp.where(slab == SLABS, 1, 0)
        for parity in range(2):
            count = ROWS[parity]
            total = dot(window_of(y_second, slab, parity), w1[K_OWN:]) + partial[slab - 1, parity, 0:count]
            total = jnp.maximum(total, 0.0) * mask[tail, parity, 0:count]
            hidden[slab, parity, 0:count] = total.astype(BF16)
        return carry

    lax.fori_loop(1, SLABS + 1, conv1, 0, unroll=7)
    for parity, count in ((0, ROWS_E), (1, 256)):
        place_in = iota((count, 256), 0) % PART
        before = hidden[SLABS, parity, 0:count].astype(F32)
        before = jnp.where(place_in == 0, 0.0, pltpu.roll(before, 1, 0))
        hidden[0, parity, 0:count] = before.astype(BF16)
        after = hidden[1, parity, 0:count].astype(F32)
        after = jnp.where(place_in == PART - 1, 0.0, pltpu.roll(after, count - 1, 0))
        hidden[SLABS + 1, parity, 0:count] = after.astype(BF16)

    def conv2(slab, carry):
        pieces = []
        for dq in range(3):
            at = slab - 1 + dq
            pieces += [hidden[at, 0, 0:256], hidden[at, 1, 0:256], hidden[at, 0, PART:ROWS_E]]
        total = dot(jnp.concatenate(pieces, axis=1), w2[...])
        x[0, slab - 1] = total[:, :128] + y_own[slab, 1, 0:256].astype(F32)
        x[1, slab - 1] = total[:, 128:] + y_own[slab, 0, PART:ROWS_E].astype(F32)
        return carry

    lax.fori_loop(1, SLABS + 1, conv2, 0, unroll=7)

    e_row = iota((SLABS * PART, 256), 0)
    e_valid = (e_row % PART) * SLABS + e_row // PART < DISP
    head_col = jnp.zeros((V, 128), F32)
    for v in range(V):
        head_col = jnp.where(iota((V, 128), 0) == v, head[v], head_col)

    def attend(quad, carry):
        at = pl.ds(pl.multiple_of(quad * PART, PART), PART)
        for half in range(2):
            tokens = jnp.concatenate([x[half, slab, at, :] for slab in range(SLABS)], axis=0)
            rounded = tokens.astype(BF16)
            turned = jnp.concatenate([tokens, jnp.zeros((PART, 128), F32)], axis=0).T
            derived = dot(derive_w[...], turned.astype(BF16)).astype(BF16)
            queries, values = derived[:128], derived[128:]
            chosen = []
            for px in range(4):
                at_px = slice(px * 32, px * 32 + 32)
                above_px = jnp.zeros((at_px.start, 128), BF16)
                below_px = jnp.zeros((128 - at_px.stop, 128), BF16)
                pieces = [above_px, queries[at_px], below_px]
                chosen.append(jnp.concatenate([k for k in pieces if k.shape[0]], axis=0))
            wide = dot(rounded, jnp.concatenate(chosen, axis=1))
            for pair in range(2):
                scores = wide[:, pair * 256 : pair * 256 + 256]
                scores = jnp.where(e_valid, scores, -1e30)
                top = jnp.max(scores, axis=0, keepdims=True)
                grown = jnp.exp(scores - top)
                scale = 1.0 / jnp.sum(grown, axis=0, keepdims=True)
                chances = (grown * scale).astype(BF16)
                chances = jnp.concatenate([chances, jnp.zeros((PART, 256), BF16)], axis=0)
                mixed = dot(values[pair * 64 : pair * 64 + 64], chances)
                for row in range(2):
                    px = pair * 2 + row
                    attended = (
                        turned[px * 32 : px * 32 + 32]
                        + mixed[row * 32 : row * 32 + 32, row * 128 : row * 128 + 128]
                    )
                    index = row * COLS + quad * 4 + half * 2 + pair
                    att[index] = attended
                    logit[pl.ds(index, 1), :] = jnp.sum(
                        attended * head_col, axis=0, keepdims=True
                    )
        return carry

    lax.fori_loop(0, 16, attend, 0, unroll=8)

    slot_lane = iota((128, 128), 1)
    depth = (slot_lane % PART) * SLABS + slot_lane // PART
    valid = (slot_lane < SLABS * PART) & (depth < DISP)
    depth_f = depth.astype(F32)
    logits = jnp.where(valid, logit[...], -1e30)
    grown = jnp.where(valid, jnp.exp(logits - jnp.max(logits, axis=1, keepdims=True)), 0.0)
    prob = grown / jnp.sum(grown, axis=1, keepdims=True)
    disparity = jnp.sum(prob * depth_f, axis=1, keepdims=True)
    disp_row = jnp.broadcast_to(disparity, (128, 128)).T[0:1]
    turned = [pltpu.roll(target[...], lax.rem(256 + row * COLS - col0, 256), 1) for row in range(2)]
    lane_row = iota((1, 128), 1)
    wanted = jnp.where(lane_row < COLS, turned[0][0:1, :128], turned[1][1:2, :128])
    residual = disp_row - wanted
    size = jnp.abs(residual)
    huber = jnp.where(size < 1.0, 0.5 * residual * residual, size - 0.5)
    pixels = 1.0 / ((row_last + 1) * (2 * 4 * COLS)).astype(F32)
    loss = jnp.sum(huber, axis=1, keepdims=True) * pixels
    slope = jnp.clip(residual, -1.0, 1.0) * pixels
    slope_col = jnp.broadcast_to(slope, (128, 128)).T
    weight[...] = slope_col * prob * (depth_f - disparity)

    def gather(block, total):
        for k in range(8):
            px = block * 8 + k
            total += att[px] * weight[pl.ds(px, 1), :]
        return total

    total = lax.fori_loop(0, 16, gather, jnp.zeros((V, 128), F32))
    padded = jnp.concatenate([total, jnp.zeros((128 - V, 128), F32)], axis=0)
    grads = jnp.sum(padded.T, axis=0, keepdims=True)
    sums = jnp.where(lane_row == V, loss, grads)
    out[...] = jnp.broadcast_to(jnp.concatenate([disp_row, sums], axis=0)[None], (128, 2, 128))


def finish_kernel(place, everyone, disparity, normals, loss, head_grad):
    row_index, row_last = place[1], place[2]
    sums = jnp.sum(everyone[...], axis=0)[1:2]
    head_grad[...] = sums[:, :V]
    loss[0, 0] = jnp.sum(jnp.where(iota((1, 128), 1) == V, sums, 0.0))
    low = iota((8, 128), 1) < COLS
    bands = []
    for band in range(2):
        start = jnp.minimum(row_index + band, row_last) * 4
        lines = [
            jnp.broadcast_to(everyone[start + k][0:1], (8, 128)) for k in range(4)
        ]
        swapped = [pltpu.roll(line, COLS, 1) for line in lines]
        tops = [jnp.where(low, lines[k], swapped[k + 1]) for k in (0, 2)]
        bottoms = [jnp.where(low, swapped[k], lines[k + 1]) for k in (0, 2)]
        bands += [jnp.concatenate(tops, axis=1), jnp.concatenate(bottoms, axis=1)]
    top, bottom, follow = bands[0], bands[1], bands[2]
    step = jnp.where(row_index < row_last, 1.0, 0.0)
    lane = iota((8, 256), 1)
    for row, (here, below, scale) in enumerate(((top, bottom, 1.0), (bottom, follow, step))):
        downward = (below - here) * scale
        across = jnp.where(lane < 255, pltpu.roll(here, 255, 1) - here, 0.0)
        inverse = 1.0 / jnp.sqrt(across * across + downward * downward + 1.0)
        disparity[0, row : row + 1, :] = here[0:1]
        normals[0, 0, row : row + 1, :] = (-across * inverse)[0:1]
        normals[1, 0, row : row + 1, :] = (-downward * inverse)[0:1]
        normals[2, 0, row : row + 1, :] = inverse[0:1]


VMEM_SPEC = pl.BlockSpec(memory_space=pltpu.VMEM)
HBM_SPEC = pl.BlockSpec(memory_space=pltpu.HBM)
SMEM_SPEC = pl.BlockSpec(memory_space=pltpu.SMEM)
PARAMS = pltpu.CompilerParams(vmem_limit_bytes=24 * 1024 * 1024)


def in_hbm(x):
    return pltpu.with_memory_space_constraint(x, pltpu.HBM)


def arr(dtype, *shape):
    return jax.ShapeDtypeStruct(shape, dtype)


def body(left, right, stem, conv, attn, head, target):
    disp_index = lax.axis_index("disp")
    row_index = lax.axis_index("rows")
    row_count = lax.axis_size("rows")
    left, right = left[0], right[0]
    place = jnp.stack([disp_index, row_index, jnp.int32(row_count - 1)]).astype(jnp.int32)
    window = pl.pallas_call(
        pack_kernel,
        out_shape=arr(BF16, 2, 224, 256),
        in_specs=[SMEM_SPEC, HBM_SPEC, HBM_SPEC],
        out_specs=VMEM_SPEC,
        scratch_shapes=[
            pltpu.VMEM((2, 224, 256), BF16),
            pltpu.VMEM((2, 224, 256), BF16),
            pltpu.SemaphoreType.DMA((2,)),
        ],
        compiler_params=PARAMS,
        name="pack",
    )(place, in_hbm(left), in_hbm(right))
    pairs = (
        [(r, (((r + 1) ^ 1) - 1) % row_count) for r in range(row_count)],
        [(r, r ^ 1) for r in range(row_count)],
    )
    first, second = [
        lax.ppermute(
            window,
            ("rows", "disp"),
            [(a * 4 + k, b * 4 + (k + 2) % 4) for a, b in pair for k in range(4)],
        )
        for pair in pairs
    ]
    y_own, partial, w1, w2, lift_w, derive_w, mask, order, pick_halo, turn_halo = pl.pallas_call(
        prep_kernel,
        out_shape=(
            arr(BF16, 9, 2, ROWS_E, 128),
            arr(F32, SLABS, 2, ROWS_E, 256),
            arr(BF16, 2 * K_OWN, 256),
            arr(BF16, 3 * K_OWN, 256),
            arr(BF16, 128, 256),
            arr(BF16, 256, 128),
            arr(F32, 2, 2, ROWS_E, 256),
            arr(BF16, 9 * PART, 128),
            arr(BF16, WIN_L * G, 256),
            arr(BF16, 256, 256),
        ),
        in_specs=[SMEM_SPEC] + [HBM_SPEC] * 5,
        out_specs=(VMEM_SPEC,) * 10,
        scratch_shapes=[
            pltpu.VMEM((2, 224, 256), BF16),
            pltpu.VMEM((2, 224, 256), BF16),
            pltpu.VMEM((54, V, V), BF16),
            pltpu.VMEM((G, V), BF16),
            pltpu.VMEM((3, V, V), BF16),
            pltpu.VMEM((2, WIN_L * G, 256), F32),
            pltpu.VMEM((K_OWN, 256), BF16),
            pltpu.SemaphoreType.DMA((5,)),
        ],
        compiler_params=PARAMS,
        cost_estimate=pl.CostEstimate(flops=6 * 10**9, bytes_accessed=4 * 10**6, transcendentals=0),
        name="prep",
    )(
        place,
        in_hbm(left),
        in_hbm(right),
        in_hbm(conv.transpose(0, 2, 3, 4, 1, 5).reshape(54, V, V)),
        in_hbm(stem.T),
        in_hbm(attn),
    )
    partial = pl.pallas_call(
        first_kernel,
        out_shape=arr(F32, SLABS, 2, ROWS_E, 256),
        in_specs=[SMEM_SPEC] + [VMEM_SPEC] * 7,
        out_specs=VMEM_SPEC,
        scratch_shapes=[
            pltpu.VMEM((2, WIN_L * G, 256), F32),
            pltpu.VMEM((9, 2, ROWS_E, 128), BF16),
        ],
        compiler_params=PARAMS,
        cost_estimate=pl.CostEstimate(flops=4 * 10**9, bytes_accessed=4 * 10**6, transcendentals=0),
        name="first",
    )(place, first, partial, w1, lift_w, order, pick_halo, turn_halo)
    shares = pl.pallas_call(
        volume_kernel,
        out_shape=arr(F32, 128, 2, 128),
        in_specs=[SMEM_SPEC] + [VMEM_SPEC] * 11 + [SMEM_SPEC, VMEM_SPEC],
        out_specs=VMEM_SPEC,
        scratch_shapes=[
            pltpu.VMEM((2, WIN_L * G, 256), F32),
            pltpu.VMEM((9, 2, ROWS_E, 128), BF16),
            pltpu.VMEM((9, 2, ROWS_E, 256), BF16),
            pltpu.VMEM((2, SLABS, 256, 128), F32),
            pltpu.VMEM((2 * COLS, V, 128), F32),
            pltpu.VMEM((2 * COLS, 128), F32),
            pltpu.VMEM((2 * COLS, 128), F32),
        ],
        compiler_params=PARAMS,
        name="volume",
    )(
        place,
        second,
        y_own,
        partial,
        w1,
        w2,
        lift_w,
        derive_w,
        mask,
        order,
        pick_halo,
        turn_halo,
        head,
        target[0],
    )
    everyone = lax.all_to_all(shares, ("rows", "disp"), 0, 0, tiled=True)
    disparity, normals, loss, head_grad = pl.pallas_call(
        finish_kernel,
        out_shape=(arr(F32, 1, 2, 256), arr(F32, 3, 1, 2, 256), arr(F32, 1, 1), arr(F32, 1, V)),
        in_specs=[SMEM_SPEC, VMEM_SPEC],
        out_specs=(VMEM_SPEC, VMEM_SPEC, SMEM_SPEC, VMEM_SPEC),
        compiler_params=PARAMS,
        name="finish",
    )(place, everyone)
    return disparity, normals, loss.reshape(()), head_grad.reshape(V)


def solution(mesh):
    rows4 = P(None, "rows", None, None)
    return jax.shard_map(
        body,
        mesh=mesh,
        in_specs=(rows4, rows4, P(), P(), P(), P(), P(None, "rows", None)),
        out_specs=(P(None, "rows", None), P(None, None, "rows", None), P(), P()),
        check_vma=False,
    )
```
